128 devices in a mesh: tm: 8 (over x, core), space: 16 (over y, z).
Axes of the slice: x: 4, y: 4, z: 4, core: 2. Of those that a mesh axis runs over, the one named last changes fastest.
Arguments:
- activations: bfloat16 [16, 64, 192, 128], P('tm', 'space')
- weight_one: bfloat16 [5184, 192], replicated, may hold values from -0.078125 to 0.078125
- weight_two: bfloat16 [5184, 192], replicated, may hold values from -0.078125 to 0.078125
- gain_one: float32 [192], replicated, may hold values from 0.1 to 1.9
- bias_one: float32 [192], replicated, may hold values from -3 to 3
- gain_two: float32 [192], replicated, may hold values from 0.1 to 1.9
- bias_two: float32 [192], replicated, may hold values from -3 to 3
- cotangent: bfloat16 [16, 64, 192, 128], P('tm', 'space'), may hold values from -6 to 6
- clip_lengths: int32 [4], replicated, may hold values from 1 to 8, as said below
Outputs:
- decoded: bfloat16 [16, 64, 192, 128], P('tm', 'space')
- input_grad: bfloat16 [16, 64, 192, 128], P('tm', 'space')
- weight_grad_one: float32 [5184, 192], P('space')
- weight_grad_two: float32 [5184, 192], P('space')
The draws below stay inside these ranges and needn't reach their ends.
Inputs may be any that keep to these rules, and one draw needn't show every extreme that they name: `clip_lengths`: the 4 clip lengths sum to 16; the last clip has exactly 8 frames and no clip is longer.
All inputs are finite; a program needn't handle non-finite values.
Results may differ from the reference program's by a relative error of at most 0.0056.
Values may be sent and summed in bfloat16 or wider, within the bound.
No kernel may reach another device: no remote copies, remote signals or barrier semaphores. Data moves between devices by JAX's collectives and lax.ppermute only.
A program may use at most 128 MiB of HBM per device.

```python
import jax
import jax.numpy as jnp
from jax import lax

C = 192
GROUPS = 32
TAPS = 27
W = 128
FRAMES = 16
HEIGHT = 64


def draw_activations(key, part):
    key = jax.random.fold_in(key, 11)
    row_index = jnp.arange(HEIGHT, dtype=jnp.float32)
    rising = jnp.exp(jnp.log(3.0) * row_index / max(HEIGHT - 1, 1))
    first_key = jax.random.fold_in(key, 0)
    values = jax.random.normal(first_key, (FRAMES, HEIGHT, C, W), jnp.float32) * rising[None, :, None, None]
    return values.astype(jnp.bfloat16)


def draw_clip_lengths(key, part):
    key = jax.random.fold_in(key, 23)
    last_length = FRAMES // 2
    remaining = FRAMES - last_length
    order = jax.random.permutation(key, remaining - 1) + 1
    low_cut = jnp.minimum(order[0], order[1]).astype(jnp.int32)
    high_cut = jnp.maximum(order[0], order[1]).astype(jnp.int32)
    lengths = jnp.stack([low_cut, high_cut - low_cut, remaining - high_cut, jnp.int32(last_length) + 0 * low_cut])
    return lengths.astype(jnp.int32)


def block_levels(stream_key, dims, cuts, least, largest):
    loudness = 1.0
    for position, shards_of in cuts:
        draws = jax.random.uniform(jax.random.fold_in(jax.random.fold_in(stream_key, 6), position), (shards_of,), jnp.float32, least / len(cuts), largest / len(cuts))
        loudness = loudness * jnp.repeat(jnp.exp(draws), dims[position] // shards_of).reshape((-1,) + (1,) * (len(dims) - 1 - position))
    return loudness


def normal_values(key, extent, scale, most, shards=(), held_as=jnp.bfloat16):
    level = block_levels(key, extent, shards, -0.22, 0.18) if shards else 1.0
    drawn = jax.random.normal(key, extent, jnp.float32) * scale * level
    return jnp.minimum(jnp.maximum(drawn, -most), most).astype(held_as)


def setup_inputs(seed: int = 0) -> dict:
    keys = jax.random.split(jax.random.key(seed), 10)
    activations = draw_activations(jax.random.fold_in(keys[9], 71), 0)
    weight_one = normal_values(keys[1], (TAPS * C, C), (TAPS * C) ** -0.5, 0.078125)
    weight_two = normal_values(keys[2], (TAPS * C, C), (TAPS * C) ** -0.5, 0.078125)
    gain_one = jnp.clip(1.0 + 0.18 * jax.random.normal(keys[3], (C,), jnp.float32), 0.1, 1.9)
    bias_one = normal_values(keys[4], (C,), 0.5, 3.0, (), jnp.float32)
    gain_two = jnp.clip(1.0 + 0.18 * jax.random.normal(keys[5], (C,), jnp.float32), 0.1, 1.9)
    bias_two = normal_values(keys[6], (C,), 0.5, 3.0, (), jnp.float32)
    cotangent = normal_values(keys[7], (FRAMES, HEIGHT, C, W), 1.0, 6.0, ((0, 8), (1, 16)))
    clip_lengths = draw_clip_lengths(jax.random.fold_in(keys[9], 71), 0)
    return dict(activations=activations, weight_one=weight_one, weight_two=weight_two, gain_one=gain_one, bias_one=bias_one, gain_two=gain_two, bias_two=bias_two, cotangent=cotangent, clip_lengths=clip_lengths)


NORM_EPSILON = 1e-05

def rounded(tensor):
    return lax.optimization_barrier(tensor.astype(jnp.bfloat16)).astype(jnp.float32)

def keep_table(frame_count, clip_ends):
    frame_ids = jnp.arange(frame_count, dtype=jnp.int32)
    own_clip = lax.optimization_barrier(jnp.sum((frame_ids[:, None] >= clip_ends[None, :]).astype(jnp.int32), axis=1))
    lagged = [jnp.ones((frame_count,), jnp.float32)]
    for lag_size in (1, 2):
        shifted_ids = frame_ids - lag_size
        before_clip = lax.optimization_barrier(jnp.sum((shifted_ids[:, None] >= clip_ends[None, :]).astype(jnp.int32), axis=1))
        allowed = (shifted_ids >= 0) & (before_clip == own_clip)
        lagged.append(allowed.astype(jnp.float32))
    return jnp.stack(lagged)

def causal_conv(active, weight, keep_rows):
    frame_count = active.shape[0]
    channels = active.shape[2]
    kernel = weight.reshape(3, 3, 3, channels, weight.shape[1])
    earlier = jnp.pad(active, ((2, 0), (0, 0), (0, 0), (0, 0)))
    summed = jnp.zeros((frame_count, active.shape[1], weight.shape[1], active.shape[3]), jnp.float32)
    for tap_index in range(3):
        lag_size = 2 - tap_index
        partial_out = lax.conv_general_dilated(earlier[tap_index:tap_index + frame_count], kernel[tap_index], (1, 1), ((1, 1), (1, 1)), dimension_numbers=('NHCW', 'HWIO', 'NHCW'), precision=lax.Precision.HIGHEST)
        summed = summed + partial_out * keep_rows[lag_size][:, None, None, None]
    return summed

def group_act(tensor, gain, bias):
    frame_count, height, channels, columns = tensor.shape
    grouped = tensor.reshape(frame_count, height, GROUPS, channels // GROUPS, columns)
    mean_value = lax.optimization_barrier(jnp.mean(grouped, axis=(1, 3, 4), keepdims=True))
    centered = grouped - mean_value
    variance = lax.optimization_barrier(jnp.mean(centered * centered, axis=(1, 3, 4), keepdims=True))
    scaled = (centered * lax.rsqrt(variance + NORM_EPSILON)).reshape(tensor.shape)
    return jax.nn.silu(scaled * gain[None, None, :, None] + bias[None, None, :, None])

def reference(activations, weight_one, weight_two, gain_one, bias_one, gain_two, bias_two, cotangent, clip_lengths):
    clip_ends = jnp.cumsum(clip_lengths).astype(jnp.int32)
    keep_rows = keep_table(FRAMES, clip_ends)
    inputs = activations.astype(jnp.float32)
    kernel_one = weight_one.astype(jnp.float32)
    kernel_two = weight_two.astype(jnp.float32)
    act_one, norm_one_adjoint = jax.vjp(lambda tensor: group_act(tensor, gain_one, bias_one), inputs)
    active_one = rounded(act_one)
    conv_one, conv_one_adjoint = jax.vjp(lambda tensor, weight: causal_conv(tensor, weight, keep_rows), active_one, kernel_one)
    act_two, norm_two_adjoint = jax.vjp(lambda tensor: group_act(tensor, gain_two, bias_two), conv_one)
    active_two = rounded(act_two)
    conv_two, conv_two_adjoint = jax.vjp(lambda tensor, weight: causal_conv(tensor, weight, keep_rows), active_two, kernel_two)
    decoded = (inputs + conv_two).astype(jnp.bfloat16)
    upstream = cotangent.astype(jnp.float32)
    grad_active_two, weight_grad_two = conv_two_adjoint(upstream)
    grad_conv_one = rounded(norm_two_adjoint(grad_active_two)[0])
    grad_active_one, weight_grad_one = conv_one_adjoint(grad_conv_one)
    grad_inputs = norm_one_adjoint(grad_active_one)[0]
    input_grad = (upstream + grad_inputs).astype(jnp.bfloat16)
    grad_scale = 1.0 / jnp.sqrt(jnp.float32(FRAMES * HEIGHT * W))
    return (decoded, input_grad, (weight_grad_one * grad_scale).astype(jnp.float32), (weight_grad_two * grad_scale).astype(jnp.float32))
```

```python
import functools

import jax
import jax.numpy as jnp
from jax import lax
from jax.experimental import pallas as pl
from jax.experimental.pallas import tpu as pltpu
from jax.sharding import PartitionSpec as P

GROUPS = 32
NORM_EPSILON = 1e-05

C = 192
W = 128
PER_GROUP = C // GROUPS
ROWS = 4
OWN = 2
TAP_ROWS = 3 * C
DEPTH = 3 * TAP_ROWS
ALL_TAPS = 3 * DEPTH
SPACE = 16
TM = 8
SHARE = ALL_TAPS // SPACE
PACKED = 512
LOCAL_COUNT = ROWS * PER_GROUP * W
FULL_COUNT = LOCAL_COUNT * SPACE

F32 = jnp.float32
BF16 = jnp.bfloat16
EXACT = lax.Precision.HIGHEST


def call(kernel, out_shape, operands, smem=0, scratch=(), flops=0, **extra):
    nbytes = sum(x.size * x.dtype.itemsize for x in operands)
    return pl.pallas_call(
        kernel,
        out_shape=out_shape,
        in_specs=[pl.BlockSpec(memory_space=pltpu.SMEM)] * smem
        + [pl.BlockSpec(memory_space=pltpu.VMEM)] * (len(operands) - smem),
        out_specs=jax.tree.map(lambda _: pl.BlockSpec(memory_space=pltpu.VMEM), out_shape),
        scratch_shapes=list(scratch),
        compiler_params=pltpu.CompilerParams(vmem_limit_bytes=48 * 1024 * 1024),
        cost_estimate=pl.CostEstimate(flops=flops, bytes_accessed=nbytes, transcendentals=0),
        **extra,
    )(*operands)


def lane_ids(rows=C):
    return lax.broadcasted_iota(jnp.int32, (rows, W), 1)


def membership():
    channel = lax.broadcasted_iota(jnp.int32, (C, W), 0)
    group = lane_ids()
    inside = (channel >= group * PER_GROUP) & (channel < (group + 1) * PER_GROUP)
    return inside.astype(F32)


def to_groups(columns):
    lanes = lane_ids()
    packed = jnp.zeros((C, W), F32)
    for i, column in enumerate(columns):
        packed = jnp.where(lanes == i, column, packed)
    summed = lax.dot_general(
        packed, membership(), (((0,), (0,)), ((), ())), precision=EXACT, preferred_element_type=F32
    )
    return summed[:8]


def to_channels(table):
    return lax.dot_general(
        membership(), table, (((1,), (1,)), ((), ())), precision=EXACT, preferred_element_type=F32
    )


def merged_stats(parts_ref, frames):
    means = parts_ref[:, 0:4, :]
    mean = jnp.sum(means, axis=0) * (1.0 / SPACE)
    spread = jnp.sum((means - mean[None]) ** 2, axis=0) * float(LOCAL_COUNT)
    variance = (jnp.sum(parts_ref[:, 4:8, :], axis=0) + spread) * (1.0 / FULL_COUNT)
    inverse = lax.rsqrt(variance + NORM_EPSILON)
    return to_channels(jnp.concatenate([mean, inverse], axis=0))


def local_stats(blocks):
    sums = []
    for rows in blocks:
        total = rows[0]()
        for row in rows[1:]:
            total = total + row()
        sums.append(jnp.sum(total, axis=1, keepdims=True))
    means = to_groups(sums) * (1.0 / LOCAL_COUNT)
    spread = to_channels(means)
    squares = []
    for f, rows in enumerate(blocks):
        total = None
        for row in rows:
            centered = row() - spread[:, f : f + 1]
            total = centered * centered if total is None else total + centered * centered
        squares.append(jnp.sum(total, axis=1, keepdims=True))
    deviations = to_groups(squares)
    return jnp.concatenate([means[:4], deviations[:4]], axis=0)


def store_shifted(cols_ref, h, f, field):
    lanes = lane_ids()
    before = jnp.where(lanes == 0, 0.0, pltpu.roll(field, 1, 1))
    after = jnp.where(lanes == W - 1, 0.0, pltpu.roll(field, W - 1, 1))
    for s, part in enumerate((before, field, after)):
        start = h * TAP_ROWS + s * C
        cols_ref[start : start + C, f * W : (f + 1) * W] = part.astype(BF16)


def conv_rows(kernels, cols_ref, factors, finish):
    wide = lax.broadcasted_iota(jnp.int32, (C, 2 * W), 1) < W
    for h in range(ROWS):
        total = None
        for k in range(3):
            part = jnp.dot(
                kernels[k],
                cols_ref[h * TAP_ROWS : h * TAP_ROWS + DEPTH, k * W : (k + 2) * W],
                preferred_element_type=F32,
            )
            if factors[k] is not None:
                part = part * jnp.where(wide, factors[k][0], factors[k][1])
            total = part if total is None else total + part
        finish(h, total)


def loader(own_ref, beside_ref, top_ref, bottom_ref, own_first, beside_row0):
    def load(f, h):
        if h == 0:
            return top_ref[beside_row0 + f].astype(F32)
        if h == ROWS + 1:
            return bottom_ref[beside_row0 + f].astype(F32)
        if own_first:
            block = own_ref[f, h - 1] if f < OWN else beside_ref[f - OWN, h - 1]
        else:
            block = beside_ref[f, h - 1] if f < OWN else own_ref[f - OWN, h - 1]
        return block.astype(F32)

    return load


def stats_kernel(own_ref, prev_ref, out_ref):
    def row(ref, f, h):
        return lambda: ref[f, h].astype(F32)

    blocks = [[row(prev_ref, f, h) for h in range(ROWS)] for f in range(OWN)]
    blocks += [[row(own_ref, f, h) for h in range(ROWS)] for f in range(OWN)]
    out_ref[...] = jnp.broadcast_to(local_stats(blocks)[None], (SPACE, 8, W))


def silu_of(pre):
    return pre / (1.0 + jnp.exp(-pre))


def conv_one_kernel(
    table_ref, parts_ref, own_ref, prev_ref, top_ref, bottom_ref, param_ref, weight_ref,
    cols_ref, conv_ref, out_ref,
):
    stats = merged_stats(parts_ref, 4)
    gain, bias = param_ref[:, 0:1], param_ref[:, 1:2]
    load = loader(own_ref, prev_ref, top_ref, bottom_ref, False, 0)
    for f in range(4):
        mean = jnp.broadcast_to(stats[:, f : f + 1], (C, W))
        scale = jnp.broadcast_to(stats[:, 4 + f : 5 + f] * gain, (C, W))
        shift = jnp.broadcast_to(bias, (C, W))
        for h in range(ROWS + 2):
            active = silu_of((load(f, h) - mean) * scale + shift)
            if h == 0:
                active = active * table_ref[12]
            if h == ROWS + 1:
                active = active * table_ref[13]
            store_shifted(cols_ref, h, f, active)
    kernels = [weight_ref[:, k * DEPTH : (k + 1) * DEPTH] for k in range(3)]
    factors = [(table_ref[(2 - k) * 4], table_ref[(2 - k) * 4 + 1]) for k in range(2)] + [None]

    def finish(h, total):
        conv_ref[0, h] = total[:, :W]
        conv_ref[1, h] = total[:, W:]

    conv_rows(kernels, cols_ref, factors, finish)

    def row(f, h):
        return lambda: conv_ref[f, h]

    blocks = [[row(f, h) for h in range(ROWS)] for f in range(OWN)]
    out_ref[...] = jnp.broadcast_to(local_stats(blocks)[None], (SPACE, 8, W))


def turn_kernel(one_ref, two_ref, out_one_ref, out_two_ref):
    for src, dst in ((one_ref, out_one_ref), (two_ref, out_two_ref)):
        for tap in range(27):
            k, spot = divmod(26 - tap, 9)
            block = src[:, tap * C : (tap + 1) * C]
            dst[k, :, spot * C : (spot + 1) * C] = block.T


def adjoint_kernel(table_ref, own_ref, next_ref, top_ref, bottom_ref, weight_ref, out_ref, cols_ref, *, first):
    load = loader(own_ref, next_ref, top_ref, bottom_ref, True, first)
    for f in range(4):
        for h in range(ROWS + 2):
            store_shifted(cols_ref, h, f, load(f, h))
    factors = [None] + [(table_ref[j * 4 + j], table_ref[j * 4 + j + 1]) for j in (1, 2)]

    def finish(h, total):
        out_ref[0, h] = total[:, :W]
        out_ref[1, h] = total[:, W:]

    conv_rows([weight_ref[j] for j in range(3)], cols_ref, factors, finish)


def norm_grad_rows(f, h, value, upstream, mean, inverse, gain, bias):
    normalized = (value - mean) * inverse
    pre = normalized * gain + bias
    sigmoid = 1.0 / (1.0 + jnp.exp(-pre))
    grad = upstream * (sigmoid * (1.0 + pre * (1.0 - sigmoid))) * gain
    return normalized, grad, pre * sigmoid


def norm_grad(load, upstream_ref, stats, first, gain, bias, grad_ref, norm_ref, active_ref):
    plain, weighted = [], []
    for f in range(OWN):
        mean = jnp.broadcast_to(stats[:, first + f : first + f + 1], (C, W))
        inverse = jnp.broadcast_to(stats[:, 4 + first + f : 5 + first + f], (C, W))
        gain_wide = jnp.broadcast_to(gain, (C, W))
        bias_wide = jnp.broadcast_to(bias, (C, W))
        sums = None
        for h in range(ROWS):
            normalized, grad, active = norm_grad_rows(
                f, h, load(f, h), upstream_ref[f, h], mean, inverse, gain_wide, bias_wide
            )
            grad_ref[f, h] = grad
            norm_ref[f, h] = normalized
            if active_ref is not None:
                active_ref[f, h] = active.astype(BF16)
            pair = (grad, grad * normalized)
            sums = pair if sums is None else (sums[0] + pair[0], sums[1] + pair[1])
        plain.append(jnp.sum(sums[0], axis=1, keepdims=True))
        weighted.append(jnp.sum(sums[1], axis=1, keepdims=True))
    return to_groups(plain + weighted)


def norm_two_kernel(parts_ref, conv_ref, upstream_ref, param_ref, active_ref, grad_ref, norm_ref, out_ref):
    stats = merged_stats(parts_ref, 2)
    sums = norm_grad(
        lambda f, h: conv_ref[f, h], upstream_ref, stats, 0, param_ref[:, 2:3], param_ref[:, 3:4],
        grad_ref, norm_ref, active_ref,
    )
    out_ref[...] = jnp.broadcast_to(sums[None], (SPACE, 8, W))


def norm_one_kernel(parts_ref, own_ref, upstream_ref, param_ref, grad_ref, norm_ref, out_ref):
    stats = merged_stats(parts_ref, 4)
    sums = norm_grad(
        lambda f, h: own_ref[f, h].astype(F32), upstream_ref, stats, 2, param_ref[:, 0:1], param_ref[:, 1:2],
        grad_ref, norm_ref, None,
    )
    out_ref[...] = jnp.broadcast_to(sums[None], (SPACE, 8, W))


def field_grad(parts_ref, sums_ref, grad_ref, norm_ref, first, finish):
    stats = merged_stats(parts_ref, 4)
    totals = to_channels(jnp.sum(sums_ref[...], axis=0) * (1.0 / FULL_COUNT))
    for f in range(OWN):
        inverse = jnp.broadcast_to(stats[:, 4 + first + f : 5 + first + f], (C, W))
        plain = jnp.broadcast_to(totals[:, f : f + 1], (C, W))
        weighted = jnp.broadcast_to(totals[:, OWN + f : OWN + f + 1], (C, W))
        for h in range(ROWS):
            finish(f, h, inverse * (grad_ref[f, h] - plain - norm_ref[f, h] * weighted))


def grad_conv_kernel(parts_ref, sums_ref, grad_ref, norm_ref, out_ref):
    def finish(f, h, value):
        out_ref[f, h] = value.astype(BF16)

    field_grad(parts_ref, sums_ref, grad_ref, norm_ref, 0, finish)


def input_grad_kernel(parts_ref, sums_ref, grad_ref, norm_ref, cot_ref, out_ref):
    def finish(f, h, value):
        out_ref[f, h] = (cot_ref[f, h].astype(F32) + value).astype(BF16)

    field_grad(parts_ref, sums_ref, grad_ref, norm_ref, 2, finish)


def weight_grad(table_ref, cols_ref, grad_ref, dense_ref, out_ref):
    wide = lax.broadcasted_iota(jnp.int32, (C, 2 * W), 1) < W
    rows = [jnp.concatenate([grad_ref[0, h], grad_ref[1, h]], axis=1) for h in range(ROWS)]
    for k in range(3):
        if k < 2:
            factor = jnp.where(wide, table_ref[(2 - k) * 4], table_ref[(2 - k) * 4 + 1])
            masked = [(row.astype(F32) * factor).astype(BF16) for row in rows]
        else:
            masked = rows
        total = None
        for h in range(ROWS):
            part = lax.dot_general(
                cols_ref[h * TAP_ROWS : h * TAP_ROWS + DEPTH, k * W : (k + 2) * W],
                masked[h],
                (((1,), (1,)), ((), ())),
                preferred_element_type=F32,
            )
            if h == 0:
                dense_ref[k * DEPTH : (k + 1) * DEPTH, :] = part
            else:
                dense_ref[k * DEPTH : (k + 1) * DEPTH, :] += part
    half = SHARE // 2
    rest = C - W
    for s in range(SPACE):
        low = dense_ref[s * SHARE : (s + 1) * SHARE, 0:W]
        high = jnp.concatenate(
            [
                dense_ref[s * SHARE : s * SHARE + half, W:C],
                dense_ref[s * SHARE + half : (s + 1) * SHARE, W:C],
            ],
            axis=1,
        )
        spare = jnp.zeros((PACKED - SHARE - half, W), F32)
        packed = jnp.concatenate([low, high, spare], axis=0).astype(out_ref.dtype)
        piece = PACKED // TM
        for i in range(TM):
            out_ref[i, s] = packed[i * piece : (i + 1) * piece]


def weight_one_kernel(table_ref, cols_ref, grad_ref, out_ref, dense_ref):
    weight_grad(table_ref, cols_ref, grad_ref, dense_ref, out_ref)


def conv_two_kernel(
    table_ref, own_ref, prev_ref, top_ref, bottom_ref, weight_ref, input_ref, cot_ref,
    decoded_ref, out_ref, cols_ref, dense_ref,
):
    load = loader(own_ref, prev_ref, top_ref, bottom_ref, False, 0)
    for f in range(4):
        for h in range(ROWS + 2):
            store_shifted(cols_ref, h, f, load(f, h))
    kernels = [weight_ref[:, k * DEPTH : (k + 1) * DEPTH] for k in range(3)]
    factors = [(table_ref[(2 - k) * 4], table_ref[(2 - k) * 4 + 1]) for k in range(2)] + [None]

    def finish(h, total):
        for f in range(OWN):
            field = input_ref[f, h].astype(F32) + total[:, f * W : (f + 1) * W]
            decoded_ref[f, h] = field.astype(BF16)

    conv_rows(kernels, cols_ref, factors, finish)
    weight_grad(table_ref, cols_ref, cot_ref, dense_ref, out_ref)


def unpack_kernel(one_ref, two_ref, out_one_ref, out_two_ref, *, scale):
    half = SHARE // 2
    for src, dst in ((one_ref, out_one_ref), (two_ref, out_two_ref)):
        dst[:, 0:W] = src[0:SHARE].astype(F32) * scale
        high = src[SHARE : SHARE + half].astype(F32) * scale
        dst[0:half, W:C] = high[:, : C - W]
        dst[half:SHARE, W:C] = high[:, C - W :]


def keep_table(first_frame, frame_count, clip_ends):
    frame_ids = first_frame + jnp.arange(frame_count, dtype=jnp.int32)
    own_clip = jnp.sum((frame_ids[:, None] >= clip_ends[None, :]).astype(jnp.int32), axis=1)
    lagged = [jnp.ones((frame_count,), F32)]
    for lag_size in (1, 2):
        shifted_ids = frame_ids - lag_size
        before_clip = jnp.sum((shifted_ids[:, None] >= clip_ends[None, :]).astype(jnp.int32), axis=1)
        allowed = (shifted_ids >= 0) & (before_clip == own_clip)
        lagged.append(allowed.astype(F32))
    return jnp.stack(lagged)


FORWARD = [(i, i + 1) for i in range(TM - 1)]
BACKWARD = [(i + 1, i) for i in range(TM - 1)]
DOWN = [(i, i + 1) for i in range(SPACE - 1)]
UP = [(i + 1, i) for i in range(SPACE - 1)]


def row_halos(first, second):
    low = jnp.concatenate([first[:, ROWS - 1], second[:, ROWS - 1]], axis=0)
    high = jnp.concatenate([first[:, 0], second[:, 0]], axis=0)
    return lax.ppermute(low, "space", DOWN), lax.ppermute(high, "space", UP)


def swap(parts):
    return lax.all_to_all(parts, "space", 0, 0)


def shape(dims, dtype=F32):
    return jax.ShapeDtypeStruct(dims, dtype)


CONV_FLOPS = 2 * OWN * ROWS * W * ALL_TAPS * C
FIELD = (OWN, ROWS, C, W)
COLS = (6 * TAP_ROWS, 4 * W)


def shards(
    activations,
    weight_one,
    weight_two,
    gain_one,
    bias_one,
    gain_two,
    bias_two,
    cotangent,
    clip_lengths,
):
    clip_ends = jnp.cumsum(clip_lengths)
    row = lax.axis_index("space")
    keeps = keep_table(lax.axis_index("tm") * OWN, 4, clip_ends)
    edges = jnp.stack([row > 0, row < SPACE - 1]).astype(F32)
    table = jnp.concatenate([keeps.reshape(-1), edges])
    params = jnp.stack([gain_one, bias_one, gain_two, bias_two], axis=1)
    turned_one, turned_two = weight_one.T, weight_two.T

    previous = lax.ppermute(activations, "tm", FORWARD)
    following = lax.ppermute(cotangent, "tm", BACKWARD)
    adjoint_one, adjoint_two = call(
        turn_kernel, (shape((3, C, DEPTH), BF16),) * 2, (turned_one, turned_two)
    )
    parts = call(stats_kernel, shape((SPACE, 8, W)), (activations, previous))
    above, below = row_halos(
        jnp.concatenate([previous, activations], axis=0), jnp.concatenate([cotangent, following], axis=0)
    )
    stats_one = swap(parts)
    columns_one, conv_one, parts = call(
        conv_one_kernel,
        (shape(COLS, BF16), shape(FIELD), shape((SPACE, 8, W))),
        (table, stats_one, activations, previous, above, below, params, turned_one),
        smem=1,
        flops=CONV_FLOPS,
    )
    grad_active_two = call(
        functools.partial(adjoint_kernel, first=4),
        shape(FIELD),
        (table, cotangent, following, above, below, adjoint_two),
        smem=1,
        scratch=[pltpu.VMEM(COLS, BF16)],
        flops=CONV_FLOPS,
    )
    stats_two = swap(parts)
    active_two, grad_norm, normalized, parts = call(
        norm_two_kernel,
        (shape(FIELD, BF16), shape(FIELD), shape(FIELD), shape((SPACE, 8, W))),
        (stats_two, conv_one, grad_active_two, params),
    )
    previous_two = lax.ppermute(active_two, "tm", FORWARD)
    sums_two = swap(parts)
    grad_conv_one = call(
        grad_conv_kernel, shape(FIELD, BF16), (stats_two, sums_two, grad_norm, normalized)
    )
    following_one = lax.ppermute(grad_conv_one, "tm", BACKWARD)
    above_two, below_two = row_halos(previous_two, active_two)
    packed = shape((TM, SPACE, PACKED // TM, W))
    local_one = call(
        weight_one_kernel,
        packed,
        (table, columns_one, grad_conv_one),
        smem=1,
        scratch=[pltpu.VMEM((ALL_TAPS, C), F32)],
        flops=CONV_FLOPS,
    )
    above_one, below_one = row_halos(grad_conv_one, following_one)
    decoded, local_two = call(
        conv_two_kernel,
        (shape(FIELD, BF16), packed),
        (table, active_two, previous_two, above_two, below_two, turned_two, activations, cotangent),
        smem=1,
        scratch=[pltpu.VMEM(COLS, BF16), pltpu.VMEM((ALL_TAPS, C), F32)],
        flops=2 * CONV_FLOPS,
    )
    rows = SPACE * PACKED // TM
    shares = [
        lax.psum_scatter(local.reshape(TM * rows, W), "tm", scatter_dimension=0, tiled=True)
        for local in (local_one, local_two)
    ]
    grad_active_one = call(
        functools.partial(adjoint_kernel, first=0),
        shape(FIELD),
        (table, grad_conv_one, following_one, above_one, below_one, adjoint_one),
        smem=1,
        scratch=[pltpu.VMEM(COLS, BF16)],
        flops=CONV_FLOPS,
    )
    grad_norm, normalized, parts = call(
        norm_one_kernel,
        (shape(FIELD), shape(FIELD), shape((SPACE, 8, W))),
        (stats_one, activations, grad_active_one, params),
    )
    sums_one = swap(parts)
    input_grad = call(
        input_grad_kernel, shape(FIELD, BF16), (stats_one, sums_one, grad_norm, normalized, cotangent)
    )
    both = jnp.concatenate([s.reshape(SPACE, PACKED // TM, W) for s in shares], axis=1).astype(BF16)
    summed = jnp.sum(swap(both).astype(F32), axis=0)
    spread = jnp.broadcast_to(summed[None], (TM,) + summed.shape)
    gathered = lax.all_to_all(spread, "tm", 0, 0).reshape(TM, 2, PACKED // TM, W)
    total_cells = OWN * TM * ROWS * SPACE * W
    share_one, share_two = call(
        functools.partial(unpack_kernel, scale=float(total_cells) ** -0.5),
        (shape((SHARE, C)),) * 2,
        (gathered[:, 0].reshape(PACKED, W), gathered[:, 1].reshape(PACKED, W)),
    )
    return (decoded, input_grad, share_one, share_two)


def solution(mesh):
    placed = (
        P("tm", "space", None, None),
        P(),
        P(),
        P(),
        P(),
        P(),
        P(),
        P("tm", "space", None, None),
        P(),
    )
    return jax.shard_map(
        shards,
        mesh=mesh,
        in_specs=placed,
        out_specs=(
            P("tm", "space", None, None),
            P("tm", "space", None, None),
            P("space", None),
            P("space", None),
        ),
        check_vma=False,
    )
```

```python
import functools

import jax
import jax.numpy as jnp
from jax import lax
from jax.experimental import pallas as pl
from jax.experimental.pallas import tpu as pltpu
from jax.sharding import PartitionSpec as P

GROUPS = 32
NORM_EPSILON = 1e-05

C = 192
W = 128
PER_GROUP = C // GROUPS
ROWS = 4
OWN = 2
TAP_ROWS = 3 * C
DEPTH = 3 * TAP_ROWS
ALL_TAPS = 3 * DEPTH
SPACE = 16
TM = 8
SHARE = ALL_TAPS // SPACE
PACKED = 512
HALF = PACKED // 2
LOCAL_COUNT = ROWS * PER_GROUP * W
FULL_COUNT = LOCAL_COUNT * SPACE

F32 = jnp.float32
BF16 = jnp.bfloat16
EXACT = lax.Precision.HIGHEST


def call(kernel, out_shape, operands, smem=0, scratch=(), flops=0, **extra):
    nbytes = sum(x.size * x.dtype.itemsize for x in operands)
    return pl.pallas_call(
        kernel,
        out_shape=out_shape,
        in_specs=[pl.BlockSpec(memory_space=pltpu.SMEM)] * smem
        + [pl.BlockSpec(memory_space=pltpu.VMEM)] * (len(operands) - smem),
        out_specs=jax.tree.map(lambda _: pl.BlockSpec(memory_space=pltpu.VMEM), out_shape),
        scratch_shapes=list(scratch),
        compiler_params=pltpu.CompilerParams(vmem_limit_bytes=48 * 1024 * 1024),
        cost_estimate=pl.CostEstimate(flops=flops, bytes_accessed=nbytes, transcendentals=0),
        **extra,
    )(*operands)


def lane_ids(rows=C):
    return lax.broadcasted_iota(jnp.int32, (rows, W), 1)


def membership():
    channel = lax.broadcasted_iota(jnp.int32, (C, W), 0)
    group = lane_ids()
    inside = (channel >= group * PER_GROUP) & (channel < (group + 1) * PER_GROUP)
    return inside.astype(F32)


def to_groups(columns):
    lanes = lane_ids()
    packed = jnp.zeros((C, W), F32)
    for i, column in enumerate(columns):
        packed = jnp.where(lanes == i, column, packed)
    summed = lax.dot_general(
        packed, membership(), (((0,), (0,)), ((), ())), precision=EXACT, preferred_element_type=F32
    )
    return summed[:8]


def to_channels(table):
    return lax.dot_general(
        membership(), table, (((1,), (1,)), ((), ())), precision=EXACT, preferred_element_type=F32
    )


def merged_stats(parts_ref):
    means = parts_ref[:, 0:4, :]
    mean = jnp.sum(means, axis=0) * (1.0 / SPACE)
    spread = jnp.sum((means - mean[None]) ** 2, axis=0) * float(LOCAL_COUNT)
    variance = (jnp.sum(parts_ref[:, 4:8, :], axis=0) + spread) * (1.0 / FULL_COUNT)
    inverse = lax.rsqrt(variance + NORM_EPSILON)
    return to_channels(jnp.concatenate([mean, inverse], axis=0))


def local_stats(blocks):
    sums = []
    for rows in blocks:
        total = rows[0]()
        for row in rows[1:]:
            total = total + row()
        sums.append(jnp.sum(total, axis=1, keepdims=True))
    means = to_groups(sums) * (1.0 / LOCAL_COUNT)
    spread = to_channels(means)
    squares = []
    for f, rows in enumerate(blocks):
        total = None
        for row in rows:
            centered = row() - spread[:, f : f + 1]
            total = centered * centered if total is None else total + centered * centered
        squares.append(jnp.sum(total, axis=1, keepdims=True))
    deviations = to_groups(squares)
    return jnp.concatenate([means[:4], deviations[:4]], axis=0)


def store_shifted(cols_ref, h, f, field):
    lanes = lane_ids()
    before = jnp.where(lanes == 0, 0.0, pltpu.roll(field, 1, 1))
    after = jnp.where(lanes == W - 1, 0.0, pltpu.roll(field, W - 1, 1))
    for s, part in enumerate((before, field, after)):
        start = h * TAP_ROWS + s * C
        cols_ref[start : start + C, f * W : (f + 1) * W] = part.astype(BF16)


def conv_rows(kernels, cols_ref, factors, finish):
    wide = lax.broadcasted_iota(jnp.int32, (C, 2 * W), 1) < W
    for h in range(ROWS):
        total = None
        for k in range(3):
            part = jnp.dot(
                kernels[k],
                cols_ref[h * TAP_ROWS : h * TAP_ROWS + DEPTH, k * W : (k + 2) * W],
                preferred_element_type=F32,
            )
            if factors[k] is not None:
                part = part * jnp.where(wide, factors[k][0], factors[k][1])
            total = part if total is None else total + part
        finish(h, total)


def edges_kernel(*refs, count):
    low_ref, high_ref = refs[count:]
    for i, ref in enumerate(refs[:count]):
        for f in range(OWN):
            low_ref[i * OWN + f] = ref[f, ROWS - 1]
            high_ref[i * OWN + f] = ref[f, 0]


def stats_kernel(own_ref, out_ref):
    def row(f, h):
        return lambda: own_ref[f, h].astype(F32)

    blocks = [[row(f, h) for h in range(ROWS)] for f in range(OWN)]
    out_ref[...] = jnp.broadcast_to(local_stats(blocks)[None], (SPACE, 8, W))


def silu_of(pre):
    return pre / (1.0 + jnp.exp(-pre))


def active_columns(cols_ref, table_ref, own_stats, prev_stats, gain, bias, own, prev, above, below):
    shift = jnp.broadcast_to(bias, (C, W))
    for f in range(4):
        stats = prev_stats if f < OWN else own_stats
        g = f % OWN
        mean = jnp.broadcast_to(stats[:, g : g + 1], (C, W))
        scale = jnp.broadcast_to(stats[:, 4 + g : 5 + g] * gain, (C, W))
        for h in range(ROWS + 2):
            if h == 0:
                field = above[f]
            elif h == ROWS + 1:
                field = below[f]
            else:
                field = (prev if f < OWN else own)[g, h - 1]
            active = silu_of((field.astype(F32) - mean) * scale + shift)
            if h == 0:
                active = active * table_ref[12]
            if h == ROWS + 1:
                active = active * table_ref[13]
            store_shifted(cols_ref, h, f, active)


def forward_conv(table_ref, weight_ref, cols_ref, finish):
    kernels = [weight_ref[:, k * DEPTH : (k + 1) * DEPTH] for k in range(3)]
    factors = [(table_ref[(2 - k) * 4], table_ref[(2 - k) * 4 + 1]) for k in range(2)] + [None]
    conv_rows(kernels, cols_ref, factors, finish)


def conv_one_kernel(
    table_ref, parts_ref, prev_parts_ref, own_ref, prev_ref, above_ref, below_ref, param_ref, weight_ref,
    cols_ref, conv_ref, half_ref, out_ref,
):
    active_columns(
        cols_ref, table_ref, merged_stats(parts_ref), merged_stats(prev_parts_ref),
        param_ref[:, 0:1], param_ref[:, 1:2], own_ref, prev_ref, above_ref, below_ref,
    )

    def finish(h, total):
        for f in range(OWN):
            field = total[:, f * W : (f + 1) * W]
            conv_ref[f, h] = field
            half_ref[f, h] = field.astype(BF16)

    forward_conv(table_ref, weight_ref, cols_ref, finish)

    def row(f, h):
        return lambda: conv_ref[f, h]

    blocks = [[row(f, h) for h in range(ROWS)] for f in range(OWN)]
    out_ref[...] = jnp.broadcast_to(local_stats(blocks)[None], (SPACE, 8, W))


def turn_kernel(src_ref, dst_ref):
    row = lax.broadcasted_iota(jnp.int32, (C, C), 0)
    eye = (row == lax.broadcasted_iota(jnp.int32, (C, C), 1)).astype(BF16)
    for tap in range(27):
        k, spot = divmod(26 - tap, 9)
        block = lax.dot_general(
            eye, src_ref[:, tap * C : (tap + 1) * C], (((1,), (1,)), ((), ())), preferred_element_type=F32
        )
        dst_ref[k, :, spot * C : (spot + 1) * C] = block.astype(BF16)


def adjoint_kernel(table_ref, own_ref, next_ref, above_ref, below_ref, weight_ref, out_ref, cols_ref, *, first):
    for f in range(4):
        for h in range(ROWS + 2):
            if h == 0:
                field = above_ref[first + f]
            elif h == ROWS + 1:
                field = below_ref[first + f]
            else:
                field = (own_ref if f < OWN else next_ref)[f % OWN, h - 1]
            store_shifted(cols_ref, h, f, field.astype(F32))
    factors = [None] + [(table_ref[j * 4 + j], table_ref[j * 4 + j + 1]) for j in (1, 2)]

    def finish(h, total):
        out_ref[0, h] = total[:, :W]
        out_ref[1, h] = total[:, W:]

    conv_rows([weight_ref[j] for j in range(3)], cols_ref, factors, finish)


def norm_grad_kernel(parts_ref, field_ref, upstream_ref, param_ref, grad_ref, norm_ref, out_ref, *, place):
    stats = merged_stats(parts_ref)
    gain = jnp.broadcast_to(param_ref[:, place : place + 1], (C, W))
    bias = jnp.broadcast_to(param_ref[:, place + 1 : place + 2], (C, W))
    plain, weighted = [], []
    for f in range(OWN):
        mean = jnp.broadcast_to(stats[:, f : f + 1], (C, W))
        inverse = jnp.broadcast_to(stats[:, 4 + f : 5 + f], (C, W))
        sums = None
        for h in range(ROWS):
            normalized = (field_ref[f, h].astype(F32) - mean) * inverse
            pre = normalized * gain + bias
            sigmoid = 1.0 / (1.0 + jnp.exp(-pre))
            grad = upstream_ref[f, h] * (sigmoid * (1.0 + pre * (1.0 - sigmoid))) * gain
            grad_ref[f, h] = grad
            norm_ref[f, h] = normalized
            pair = (grad, grad * normalized)
            sums = pair if sums is None else (sums[0] + pair[0], sums[1] + pair[1])
        plain.append(jnp.sum(sums[0], axis=1, keepdims=True))
        weighted.append(jnp.sum(sums[1], axis=1, keepdims=True))
    out_ref[...] = jnp.broadcast_to(to_groups(plain + weighted)[None], (SPACE, 8, W))


def field_grad(parts_ref, sums_ref, grad_ref, norm_ref, finish):
    stats = merged_stats(parts_ref)
    totals = to_channels(jnp.sum(sums_ref[...], axis=0) * (1.0 / FULL_COUNT))
    for f in range(OWN):
        inverse = jnp.broadcast_to(stats[:, 4 + f : 5 + f], (C, W))
        plain = jnp.broadcast_to(totals[:, f : f + 1], (C, W))
        weighted = jnp.broadcast_to(totals[:, OWN + f : OWN + f + 1], (C, W))
        for h in range(ROWS):
            finish(f, h, inverse * (grad_ref[f, h] - plain - norm_ref[f, h] * weighted))


def grad_conv_kernel(parts_ref, sums_ref, grad_ref, norm_ref, out_ref):
    def finish(f, h, value):
        out_ref[f, h] = value.astype(BF16)

    field_grad(parts_ref, sums_ref, grad_ref, norm_ref, finish)


def input_grad_kernel(parts_ref, sums_ref, grad_ref, norm_ref, cot_ref, out_ref):
    def finish(f, h, value):
        out_ref[f, h] = (cot_ref[f, h].astype(F32) + value).astype(BF16)

    field_grad(parts_ref, sums_ref, grad_ref, norm_ref, finish)


def weight_grad(table_ref, core_ref, cols_ref, grad_ref, kept_ref, send_ref, dense_ref, turned_ref):
    for h in range(ROWS):
        for f in range(OWN):
            block = grad_ref[f, h].T
            start = (h * OWN + f) * W
            turned_ref[2, start : start + W, :] = block
            wide = block.astype(F32)
            for k in range(2):
                turned_ref[k, start : start + W, :] = (wide * table_ref[(2 - k) * 4 + f]).astype(BF16)
    for k in range(3):
        for spot in range(9):
            start = spot * C
            rows = [
                cols_ref[h * TAP_ROWS + start : h * TAP_ROWS + start + C, k * W : (k + 2) * W]
                for h in range(ROWS)
            ]
            dense_ref[k * DEPTH + start : k * DEPTH + start + C, :] = jnp.dot(
                jnp.concatenate(rows, axis=1), turned_ref[k], preferred_element_type=F32
            )
    half = SHARE // 2
    first = core_ref[0] == 0
    for s in range(SPACE):
        low = dense_ref[s * SHARE : (s + 1) * SHARE, 0:W]
        high = jnp.concatenate(
            [
                dense_ref[s * SHARE : s * SHARE + half, W:C],
                dense_ref[s * SHARE + half : (s + 1) * SHARE, W:C],
            ],
            axis=1,
        )
        spare = jnp.zeros((PACKED - SHARE - half, W), F32)
        packed = jnp.concatenate([low, high, spare], axis=0).astype(BF16)
        kept_ref[s] = jnp.where(first, packed[:HALF], packed[HALF:])
        send_ref[s] = jnp.where(first, packed[HALF:], packed[:HALF])


def weight_one_kernel(table_ref, core_ref, cols_ref, grad_ref, kept_ref, send_ref, dense_ref, turned_ref):
    weight_grad(table_ref, core_ref, cols_ref, grad_ref, kept_ref, send_ref, dense_ref, turned_ref)


def conv_two_kernel(
    table_ref, core_ref, parts_ref, prev_parts_ref, own_ref, prev_ref, above_ref, below_ref, param_ref, weight_ref,
    input_ref, cot_ref, decoded_ref, kept_ref, send_ref, cols_ref, dense_ref, turned_ref,
):
    active_columns(
        cols_ref, table_ref, merged_stats(parts_ref), merged_stats(prev_parts_ref),
        param_ref[:, 2:3], param_ref[:, 3:4], own_ref, prev_ref, above_ref, below_ref,
    )

    def finish(h, total):
        for f in range(OWN):
            field = input_ref[f, h].astype(F32) + total[:, f * W : (f + 1) * W]
            decoded_ref[f, h] = field.astype(BF16)

    forward_conv(table_ref, weight_ref, cols_ref, finish)
    weight_grad(table_ref, core_ref, cols_ref, cot_ref, kept_ref, send_ref, dense_ref, turned_ref)


def add_kernel(kept_ref, came_ref, out_ref):
    out_ref[...] = (kept_ref[...].astype(F32) + came_ref[...].astype(F32)).astype(BF16)


def gather_kernel(parts_ref, out_ref):
    total = parts_ref[0].astype(F32)
    for s in range(1, SPACE):
        total = total + parts_ref[s].astype(F32)
    total = total.astype(BF16)
    for i in range(TM):
        out_ref[i] = total


def unpack_kernel(parts_ref, out_ref, *, scale):
    halves = []
    for core in range(2):
        total = parts_ref[core].astype(F32)
        for i in range(2 + core, TM, 2):
            total = total + parts_ref[i].astype(F32)
        halves.append(total * scale)
    packed = jnp.concatenate(halves, axis=0)
    half = SHARE // 2
    low = packed[0:SHARE]
    high = packed[SHARE : SHARE + half]
    out_ref[0:W, :] = low.T
    out_ref[W:C, 0:half] = high[:, : C - W].T
    out_ref[W:C, half:SHARE] = high[:, C - W :].T


def keep_table(first_frame, frame_count, clip_ends):
    frame_ids = first_frame + jnp.arange(frame_count, dtype=jnp.int32)
    own_clip = jnp.sum((frame_ids[:, None] >= clip_ends[None, :]).astype(jnp.int32), axis=1)
    lagged = [jnp.ones((frame_count,), F32)]
    for lag_size in (1, 2):
        shifted_ids = frame_ids - lag_size
        before_clip = jnp.sum((shifted_ids[:, None] >= clip_ends[None, :]).astype(jnp.int32), axis=1)
        allowed = (shifted_ids >= 0) & (before_clip == own_clip)
        lagged.append(allowed.astype(F32))
    return jnp.stack(lagged)


FORWARD = [(i, i + 1) for i in range(TM - 1)]
BACKWARD = [(i + 1, i) for i in range(TM - 1)]
DOWN = [(i, i + 1) for i in range(SPACE - 1)]
UP = [(i + 1, i) for i in range(SPACE - 1)]


SIBLING = [(i, i ^ 1) for i in range(TM)]


def row_halos(*blocks):
    rows = shape((OWN * len(blocks), C, W), BF16)
    low, high = call(functools.partial(edges_kernel, count=len(blocks)), (rows, rows), blocks)
    return lax.ppermute(low, "space", DOWN), lax.ppermute(high, "space", UP)


def swap(parts):
    return lax.all_to_all(parts, "space", 0, 0)


def shape(dims, dtype=F32):
    return jax.ShapeDtypeStruct(dims, dtype)


CONV_FLOPS = 2 * OWN * ROWS * W * ALL_TAPS * C
FIELD = (OWN, ROWS, C, W)
COLS = (6 * TAP_ROWS, 4 * W)


def shards(
    activations,
    weight_one,
    weight_two,
    gain_one,
    bias_one,
    gain_two,
    bias_two,
    cotangent,
    clip_lengths,
):
    clip_ends = jnp.cumsum(clip_lengths)
    row = lax.axis_index("space")
    keeps = keep_table(lax.axis_index("tm") * OWN, 4, clip_ends)
    edges = jnp.stack([row > 0, row < SPACE - 1]).astype(F32)
    table = jnp.concatenate([keeps.reshape(-1), edges])
    core = (lax.axis_index("tm") % 2).astype(jnp.int32).reshape(1)
    params = jnp.stack([gain_one, bias_one, gain_two, bias_two], axis=1)
    turned_one, turned_two = weight_one.T, weight_two.T
    payload = shape((SPACE, 8, W))

    previous = lax.ppermute(activations, "tm", FORWARD)
    following = lax.ppermute(cotangent, "tm", BACKWARD)
    stats_one = swap(call(stats_kernel, payload, (activations,)))
    above, below = row_halos(previous, activations, cotangent, following)
    earlier_one = lax.ppermute(stats_one, "tm", FORWARD)
    adjoint_two = call(turn_kernel, shape((3, C, DEPTH), BF16), (turned_two,))
    columns_one, conv_one, half_one, parts = call(
        conv_one_kernel,
        (shape(COLS, BF16), shape(FIELD), shape(FIELD, BF16), payload),
        (table, stats_one, earlier_one, activations, previous, above, below, params, turned_one),
        smem=1,
        flops=CONV_FLOPS,
    )
    stats_two = swap(parts)
    previous_two = lax.ppermute(half_one, "tm", FORWARD)
    above_two, below_two = row_halos(previous_two, half_one)
    grad_active_two = call(
        functools.partial(adjoint_kernel, first=4),
        shape(FIELD),
        (table, cotangent, following, above, below, adjoint_two),
        smem=1,
        scratch=[pltpu.VMEM(COLS, BF16)],
        flops=CONV_FLOPS,
    )
    earlier_two = lax.ppermute(stats_two, "tm", FORWARD)
    grad_norm, normalized, parts = call(
        functools.partial(norm_grad_kernel, place=2),
        (shape(FIELD), shape(FIELD), payload),
        (stats_two, conv_one, grad_active_two, params),
    )
    sums_two = swap(parts)
    packed = shape((SPACE, HALF, W), BF16)
    dense = [pltpu.VMEM((ALL_TAPS, C), F32), pltpu.VMEM((3, OWN * ROWS * W, C), BF16)]
    decoded, kept_two, sent_two = call(
        conv_two_kernel,
        (shape(FIELD, BF16), packed, packed),
        (
            table, core, stats_two, earlier_two, conv_one, previous_two, above_two, below_two, params, turned_two,
            activations, cotangent,
        ),
        smem=2,
        scratch=[pltpu.VMEM(COLS, BF16)] + dense,
        flops=2 * CONV_FLOPS,
    )
    grad_conv_one = call(
        grad_conv_kernel, shape(FIELD, BF16), (stats_two, sums_two, grad_norm, normalized)
    )
    following_one = lax.ppermute(grad_conv_one, "tm", BACKWARD)
    kept_one, sent_one = call(
        weight_one_kernel,
        (packed, packed),
        (table, core, columns_one, grad_conv_one),
        smem=2,
        scratch=dense,
        flops=CONV_FLOPS,
    )
    above_one, below_one = row_halos(grad_conv_one, following_one)
    adjoint_one = call(turn_kernel, shape((3, C, DEPTH), BF16), (turned_one,))
    grad_active_one = call(
        functools.partial(adjoint_kernel, first=0),
        shape(FIELD),
        (table, grad_conv_one, following_one, above_one, below_one, adjoint_one),
        smem=1,
        scratch=[pltpu.VMEM(COLS, BF16)],
        flops=CONV_FLOPS,
    )
    grad_norm, normalized, parts = call(
        functools.partial(norm_grad_kernel, place=0),
        (shape(FIELD), shape(FIELD), payload),
        (stats_one, activations, grad_active_one, params),
    )
    sums_one = swap(parts)
    input_grad = call(
        input_grad_kernel, shape(FIELD, BF16), (stats_one, sums_one, grad_norm, normalized, cotangent)
    )
    total_cells = OWN * TM * ROWS * SPACE * W
    shares = []
    for kept, sent in ((kept_one, sent_one), (kept_two, sent_two)):
        pair = call(add_kernel, packed, (kept, lax.ppermute(sent, "tm", SIBLING)))
        spread = call(gather_kernel, shape((TM, HALF, W), BF16), (swap(pair),))
        share = call(
            functools.partial(unpack_kernel, scale=float(total_cells) ** -0.5),
            shape((C, SHARE)),
            (lax.all_to_all(spread, "tm", 0, 0),),
        )
        shares.append(share.T)
    return (decoded, input_grad, shares[0], shares[1])


def solution(mesh):
    placed = (
        P("tm", "space", None, None),
        P(),
        P(),
        P(),
        P(),
        P(),
        P(),
        P("tm", "space", None, None),
        P(),
    )
    return jax.shard_map(
        shards,
        mesh=mesh,
        in_specs=placed,
        out_specs=(
            P("tm", "space", None, None),
            P("tm", "space", None, None),
            P("space", None),
            P("space", None),
        ),
        check_vma=False,
    )
```

```python
import functools

import jax
import jax.numpy as jnp
from jax import lax
from jax.experimental import pallas as pl
from jax.experimental.pallas import tpu as pltpu
from jax.sharding import PartitionSpec as P

GROUPS = 32
NORM_EPSILON = 1e-05

C = 192
W = 128
PER_GROUP = C // GROUPS
ROWS = 4
OWN = 2
TAP_ROWS = 3 * C
DEPTH = 3 * TAP_ROWS
ALL_TAPS = 3 * DEPTH
SPACE = 16
TM = 8
CLIPS = 4
SHARE = ALL_TAPS // SPACE
PACKED = 512
HALF = PACKED // 2
CHIPS = TM // 2
PIECE = HALF // CHIPS
LOCAL_COUNT = ROWS * PER_GROUP * W
FULL_COUNT = LOCAL_COUNT * SPACE

F32 = jnp.float32
BF16 = jnp.bfloat16
EXACT = lax.Precision.HIGHEST


def call(kernel, out_shape, operands, scratch=(), after=(), limit=8):
    count, extra = len(operands), len(after)

    def body(*refs):
        kernel(*refs[:count], *refs[count + extra :])

    return pl.pallas_call(
        body,
        out_shape=out_shape,
        in_specs=[pl.BlockSpec(memory_space=pltpu.VMEM)] * count + [pl.BlockSpec(memory_space=pl.ANY)] * extra,
        out_specs=jax.tree.map(lambda _: pl.BlockSpec(memory_space=pltpu.VMEM), out_shape),
        scratch_shapes=list(scratch),
        compiler_params=pltpu.CompilerParams(vmem_limit_bytes=limit * 1024 * 1024),
        cost_estimate=pl.CostEstimate(flops=0, bytes_accessed=0, transcendentals=0),
    )(*operands, *after)


def lane_ids(rows=C):
    return lax.broadcasted_iota(jnp.int32, (rows, W), 1)


def membership():
    channel = lax.broadcasted_iota(jnp.int32, (C, W), 0)
    group = lane_ids()
    inside = (channel >= group * PER_GROUP) & (channel < (group + 1) * PER_GROUP)
    return inside.astype(F32)


def to_groups(columns):
    lanes = lane_ids()
    packed = jnp.zeros((C, W), F32)
    for i, column in enumerate(columns):
        packed = jnp.where(lanes == i, column, packed)
    summed = lax.dot_general(
        packed, membership(), (((0,), (0,)), ((), ())), precision=EXACT, preferred_element_type=F32
    )
    return summed[:8]


def to_channels(table):
    return lax.dot_general(
        membership(), table, (((1,), (1,)), ((), ())), precision=EXACT, preferred_element_type=F32
    )


def merge(parts, count):
    mean = sum(part[0:4] for part in parts) * (1.0 / len(parts))
    spread = sum((part[0:4] - mean) ** 2 for part in parts) * float(count)
    return mean, sum(part[4:8] for part in parts) + spread


def stats_table(mean, squares):
    return jnp.concatenate([mean, lax.rsqrt(squares * (1.0 / FULL_COUNT) + NORM_EPSILON)], axis=0)


def local_stats(blocks):
    sums = []
    for rows in blocks:
        total = rows[0]()
        for row in rows[1:]:
            total = total + row()
        sums.append(jnp.sum(total, axis=1, keepdims=True))
    means = to_groups(sums) * (1.0 / LOCAL_COUNT)
    spread = to_channels(means)
    squares = []
    for f, rows in enumerate(blocks):
        total = None
        for row in rows:
            centered = row() - spread[:, f : f + 1]
            total = centered * centered if total is None else total + centered * centered
        squares.append(jnp.sum(total, axis=1, keepdims=True))
    deviations = to_groups(squares)
    return jnp.concatenate([means[:4], deviations[:4]], axis=0)


def store_shifted(cols_ref, h, f, field):
    lanes = lane_ids()
    before = jnp.where(lanes == 0, 0.0, pltpu.roll(field, 1, 1))
    after = jnp.where(lanes == W - 1, 0.0, pltpu.roll(field, W - 1, 1))
    for s, part in enumerate((before, field, after)):
        start = h * TAP_ROWS + s * C
        cols_ref[start : start + C, f * W : (f + 1) * W] = part.astype(BF16)


def conv_rows(kernels, cols_ref, factors, finish):
    for h in range(ROWS):
        total = None
        for k in range(3):
            part = jnp.dot(
                kernels[k],
                cols_ref[h * TAP_ROWS : h * TAP_ROWS + DEPTH, k * W : (k + 2) * W],
                preferred_element_type=F32,
            )
            if factors[k] is not None:
                part = part * factors[k]
            total = part if total is None else total + part
        finish(h, total)


def factor(table_ref, lag, frame):
    at = lag * 4 + frame
    return jnp.concatenate([table_ref[at : at + 1, :], table_ref[at + 1 : at + 2, :]], axis=1)


def edges_kernel(table_ref, *refs):
    odd = jnp.broadcast_to(table_ref[15:16, :], (C, W)) > 0.5
    inner_ref, outer_ref = refs[-2:]
    for i, ref in enumerate(refs[:-2]):
        for f in range(OWN):
            low, high = ref[f, ROWS - 1].astype(F32), ref[f, 0].astype(F32)
            inner_ref[i * OWN + f] = jnp.where(odd, high, low).astype(BF16)
            outer_ref[i * OWN + f] = jnp.where(odd, low, high).astype(BF16)


def beside(table_ref, inner_ref, outer_ref, i):
    odd = jnp.broadcast_to(table_ref[15:16, :], (C, W)) > 0.5
    inner, outer = inner_ref[i].astype(F32), outer_ref[i].astype(F32)
    above = jnp.where(odd, inner, outer) * table_ref[12:13, :]
    below = jnp.where(odd, outer, inner) * table_ref[13:14, :]
    return above, below


def stats_kernel(own_ref, prev_ref, out_ref):
    def row(ref, f, h):
        return lambda: ref[f, h].astype(F32)

    blocks = [[row(ref, f, h) for h in range(ROWS)] for ref in (prev_ref, own_ref) for f in range(OWN)]
    out_ref[...] = local_stats(blocks)


def silu_of(pre):
    return pre / (1.0 + jnp.exp(-pre))


def active_columns(cols_ref, table_ref, stats, gain, bias, own, prev, inner, outer):
    shift = jnp.broadcast_to(bias, (C, W))
    for f in range(4):
        mean = jnp.broadcast_to(stats[f][0], (C, W))
        scale = jnp.broadcast_to(stats[f][1] * gain, (C, W))
        ends = beside(table_ref, inner, outer, f)
        for h in range(ROWS + 2):
            if h == 0:
                field = ends[0]
            elif h == ROWS + 1:
                field = ends[1]
            else:
                field = (prev if f < OWN else own)[f % OWN, h - 1].astype(F32)
            active = silu_of((field - mean) * scale + shift)
            if h == 0:
                active = active * table_ref[12:13, :]
            if h == ROWS + 1:
                active = active * table_ref[13:14, :]
            store_shifted(cols_ref, h, f, active)


def forward_conv(table_ref, weight_ref, cols_ref, finish):
    kernels = [weight_ref[:, k * DEPTH : (k + 1) * DEPTH] for k in range(3)]
    factors = [factor(table_ref, 2 - k, 0) for k in range(2)] + [None]
    conv_rows(kernels, cols_ref, factors, finish)


def conv_one_kernel(
    table_ref, part_ref, a_ref, b_ref, c_ref, own_ref, prev_ref, inner_ref, outer_ref, param_ref, weight_ref,
    cols_ref, conv_ref, stats_ref, out_ref,
):
    parts = [ref[...] for ref in (part_ref, a_ref, b_ref, c_ref)]
    merged = stats_table(*merge(parts, 4 * LOCAL_COUNT))
    stats_ref[...] = merged
    wide = to_channels(merged)
    stats = [(wide[:, f : f + 1], wide[:, 4 + f : 5 + f]) for f in range(4)]
    active_columns(
        cols_ref, table_ref, stats, param_ref[:, 0:1], param_ref[:, 1:2], own_ref, prev_ref, inner_ref, outer_ref
    )

    def finish(h, total):
        for f in range(OWN):
            conv_ref[f, h] = total[:, f * W : (f + 1) * W]

    forward_conv(table_ref, weight_ref, cols_ref, finish)

    def row(f, h):
        return lambda: conv_ref[f, h]

    out_ref[...] = local_stats([[row(f, h) for h in range(ROWS)] for f in range(OWN)])


def half_kernel(src_ref, out_ref):
    out_ref[...] = src_ref[...].astype(BF16)


def merge_kernel(own_ref, a_ref, b_ref, c_ref, out_ref):
    mean, squares = merge([ref[...] for ref in (own_ref, a_ref, b_ref, c_ref)], LOCAL_COUNT)
    out_ref[...] = jnp.concatenate([mean, squares], axis=0)


def sum_kernel(own_ref, a_ref, b_ref, c_ref, out_ref):
    out_ref[...] = own_ref[...] + a_ref[...] + b_ref[...] + c_ref[...]


def turn(src_ref, dst_ref):
    row = lax.broadcasted_iota(jnp.int32, (C, C), 0)
    eye = (row == lax.broadcasted_iota(jnp.int32, (C, C), 1)).astype(BF16)
    for tap in range(27):
        k, spot = divmod(26 - tap, 9)
        block = lax.dot_general(
            eye, src_ref[:, tap * C : (tap + 1) * C], (((1,), (1,)), ((), ())), preferred_element_type=F32
        )
        dst_ref[k, :, spot * C : (spot + 1) * C] = block.astype(BF16)


def adjoint(table_ref, own_ref, next_ref, inner_ref, outer_ref, weight_ref, out_ref, cols_ref, turned_ref, first):
    turn(weight_ref, turned_ref)
    for f in range(4):
        ends = beside(table_ref, inner_ref, outer_ref, first + f)
        for h in range(ROWS + 2):
            if h == 0:
                field = ends[0]
            elif h == ROWS + 1:
                field = ends[1]
            else:
                field = (own_ref if f < OWN else next_ref)[f % OWN, h - 1].astype(F32)
            store_shifted(cols_ref, h, f, field)
    factors = [None] + [factor(table_ref, j, j) for j in (1, 2)]

    def finish(h, total):
        out_ref[0, h] = total[:, :W]
        out_ref[1, h] = total[:, W:]

    conv_rows([turned_ref[j] for j in range(3)], cols_ref, factors, finish)


def adjoint_two_kernel(
    table_ref, own_ref, next_ref, inner_ref, outer_ref, weight_ref, out_ref, cols_ref, turned_ref
):
    adjoint(table_ref, own_ref, next_ref, inner_ref, outer_ref, weight_ref, out_ref, cols_ref, turned_ref, 4)


def adjoint_one_kernel(
    table_ref, own_ref, next_ref, inner_ref, outer_ref, weight_ref, stats_ref, field_ref, param_ref,
    grad_ref, out_ref, cols_ref, turned_ref, upstream_ref,
):
    adjoint(
        table_ref, own_ref, next_ref, inner_ref, outer_ref, weight_ref, upstream_ref, cols_ref, turned_ref, 0
    )
    wide = to_channels(stats_ref[...])
    stats = [(wide[:, 2 + f : 3 + f], wide[:, 6 + f : 7 + f]) for f in range(OWN)]
    out_ref[...] = norm_grad(stats, field_ref, upstream_ref, param_ref, grad_ref, 0)


def norm_grad(stats, field_ref, upstream_ref, param_ref, grad_ref, place):
    gain = jnp.broadcast_to(param_ref[:, place : place + 1], (C, W))
    bias = jnp.broadcast_to(param_ref[:, place + 1 : place + 2], (C, W))
    plain, weighted = [], []
    for f in range(OWN):
        mean = jnp.broadcast_to(stats[f][0], (C, W))
        inverse = jnp.broadcast_to(stats[f][1], (C, W))
        sums = None
        for h in range(ROWS):
            normalized = (field_ref[f, h].astype(F32) - mean) * inverse
            pre = normalized * gain + bias
            sigmoid = 1.0 / (1.0 + jnp.exp(-pre))
            grad = upstream_ref[f, h] * (sigmoid * (1.0 + pre * (1.0 - sigmoid))) * gain
            grad_ref[f, h] = grad
            pair = (grad, grad * normalized)
            sums = pair if sums is None else (sums[0] + pair[0], sums[1] + pair[1])
        plain.append(jnp.sum(sums[0], axis=1, keepdims=True))
        weighted.append(jnp.sum(sums[1], axis=1, keepdims=True))
    return to_groups(plain + weighted)


def norm_two_kernel(
    own_ref, a_ref, b_ref, c_ref, field_ref, upstream_ref, param_ref, grad_ref, stats_ref, out_ref
):
    parts = [ref[...] for ref in (own_ref, a_ref, b_ref, c_ref)]
    merged = stats_table(*merge(parts, 4 * LOCAL_COUNT))
    stats_ref[...] = merged
    wide = to_channels(merged)
    stats = [(wide[:, f : f + 1], wide[:, 4 + f : 5 + f]) for f in range(OWN)]
    out_ref[...] = norm_grad(stats, field_ref, upstream_ref, param_ref, grad_ref, 2)


def field_grad(stats, sums, grad_ref, field_ref, finish):
    totals = to_channels(sums * (1.0 / FULL_COUNT))
    for f in range(OWN):
        mean = jnp.broadcast_to(stats[f][0], (C, W))
        inverse = jnp.broadcast_to(stats[f][1], (C, W))
        plain = jnp.broadcast_to(totals[:, f : f + 1], (C, W))
        weighted = jnp.broadcast_to(totals[:, OWN + f : OWN + f + 1], (C, W))
        for h in range(ROWS):
            normalized = (field_ref[f, h].astype(F32) - mean) * inverse
            finish(f, h, inverse * (grad_ref[f, h] - plain - normalized * weighted))


def grad_conv_kernel(stats_ref, own_ref, a_ref, b_ref, c_ref, grad_ref, field_ref, out_ref):
    def finish(f, h, value):
        out_ref[f, h] = value.astype(BF16)

    wide = to_channels(stats_ref[...])
    stats = [(wide[:, f : f + 1], wide[:, 4 + f : 5 + f]) for f in range(OWN)]
    field_grad(stats, own_ref[...] + a_ref[...] + b_ref[...] + c_ref[...], grad_ref, field_ref, finish)


def input_grad_kernel(stats_ref, own_ref, a_ref, b_ref, c_ref, grad_ref, field_ref, cot_ref, out_ref):
    def finish(f, h, value):
        out_ref[f, h] = (cot_ref[f, h].astype(F32) + value).astype(BF16)

    wide = to_channels(stats_ref[...])
    stats = [(wide[:, 2 + f : 3 + f], wide[:, 6 + f : 7 + f]) for f in range(OWN)]
    field_grad(stats, own_ref[...] + a_ref[...] + b_ref[...] + c_ref[...], grad_ref, field_ref, finish)


def weight_grad(table_ref, cols_ref, grad_ref, kept_ref, send_ref, dense_ref, turned_ref):
    for h in range(ROWS):
        for f in range(OWN):
            block = grad_ref[f, h].T
            start = (h * OWN + f) * W
            turned_ref[2, start : start + W, :] = block
            wide = block.astype(F32)
            for k in range(2):
                at = (2 - k) * 4 + f
                turned_ref[k, start : start + W, :] = (wide * table_ref[at : at + 1, 0:1]).astype(BF16)
    for k in range(3):
        for spot in range(9):
            start = spot * C
            rows = [
                cols_ref[h * TAP_ROWS + start : h * TAP_ROWS + start + C, k * W : (k + 2) * W]
                for h in range(ROWS)
            ]
            dense_ref[k * DEPTH + start : k * DEPTH + start + C, :] = jnp.dot(
                jnp.concatenate(rows, axis=1), turned_ref[k], preferred_element_type=F32
            )
    half = SHARE // 2
    first = jnp.broadcast_to(table_ref[14:15, :], (HALF, W)) < 0.5
    for s in range(SPACE):
        low = dense_ref[s * SHARE : (s + 1) * SHARE, 0:W]
        high = jnp.concatenate(
            [
                dense_ref[s * SHARE : s * SHARE + half, W:C],
                dense_ref[s * SHARE + half : (s + 1) * SHARE, W:C],
            ],
            axis=1,
        )
        spare = jnp.zeros((PACKED - SHARE - half, W), F32)
        packed = jnp.concatenate([low, high, spare], axis=0).astype(BF16)
        kept_ref[s] = jnp.where(first, packed[:HALF], packed[HALF:])
        send_ref[s] = jnp.where(first, packed[HALF:], packed[:HALF])


def weight_one_kernel(table_ref, cols_ref, grad_ref, kept_ref, send_ref, dense_ref, turned_ref):
    weight_grad(table_ref, cols_ref, grad_ref, kept_ref, send_ref, dense_ref, turned_ref)


def conv_two_kernel(
    table_ref, stats_ref, prev_stats_ref, own_ref, prev_ref, inner_ref, outer_ref, param_ref, weight_ref,
    input_ref, cot_ref, decoded_ref, kept_ref, send_ref, done_ref, cols_ref, dense_ref, turned_ref,
):
    stats = []
    for ref in (prev_stats_ref, stats_ref):
        wide = to_channels(ref[...])
        stats += [(wide[:, f : f + 1], wide[:, 4 + f : 5 + f]) for f in range(OWN)]
    active_columns(
        cols_ref, table_ref, stats, param_ref[:, 2:3], param_ref[:, 3:4], own_ref, prev_ref, inner_ref, outer_ref
    )

    def finish(h, total):
        for f in range(OWN):
            field = input_ref[f, h].astype(F32) + total[:, f * W : (f + 1) * W]
            decoded_ref[f, h] = field.astype(BF16)

    forward_conv(table_ref, weight_ref, cols_ref, finish)
    weight_grad(table_ref, cols_ref, cot_ref, kept_ref, send_ref, dense_ref, turned_ref)
    done_ref[...] = jnp.zeros((8, W), F32)


def pair_kernel(kept_one_ref, came_one_ref, kept_two_ref, came_two_ref, out_ref, done_ref):
    for i, (kept, came) in enumerate(((kept_one_ref, came_one_ref), (kept_two_ref, came_two_ref))):
        for x in range(CHIPS):
            rows = slice(x * PIECE, (x + 1) * PIECE)
            total = kept[:, rows].astype(F32) + came[:, rows].astype(F32)
            out_ref[x * SPACE : (x + 1) * SPACE, i * PIECE : (i + 1) * PIECE] = total.astype(BF16)
    done_ref[...] = jnp.zeros((8, W), F32)


def gather_kernel(parts_ref, out_ref):
    total = parts_ref[0].astype(F32)
    for s in range(1, CHIPS * SPACE):
        total = total + parts_ref[s].astype(F32)
    total = total.astype(BF16)
    for i in range(TM):
        out_ref[i] = total


def unpack_kernel(parts_ref, one_ref, two_ref, *, scale):
    half = SHARE // 2
    for i, out_ref in enumerate((one_ref, two_ref)):
        pieces = [
            parts_ref[2 * x + core, i * PIECE : (i + 1) * PIECE].astype(F32)
            for core in range(2)
            for x in range(CHIPS)
        ]
        packed = jnp.concatenate(pieces, axis=0) * scale
        high = packed[SHARE : SHARE + half]
        out_ref[0:W, :] = packed[0:SHARE].T
        out_ref[W:C, 0:half] = high[:, : C - W].T
        out_ref[W:C, half:SHARE] = high[:, C - W :].T


def table_kernel(lengths_ref, out_ref):
    place, row = lax.axis_index("tm"), lax.axis_index("space")
    ends, end = [], 0
    for i in range(CLIPS):
        end = end + lengths_ref[i]
        ends.append(end)

    def clip_of(frame):
        return sum((frame >= end).astype(jnp.int32) for end in ends)

    values = []
    for lag in range(3):
        for f in range(4):
            frame = place * OWN + f
            kept = (frame >= lag) & (clip_of(frame - lag) == clip_of(frame))
            values.append(kept.astype(F32) if lag else jnp.float32(1.0))
    flags = (row > 0, row < SPACE - 1, place % 2 > 0, row % 2 > 0)
    for i, value in enumerate(values + [flag.astype(F32) for flag in flags]):
        out_ref[i : i + 1, :] = jnp.full((1, W), value, F32)


FORWARD = [(i, i + 1) for i in range(TM - 1)]
BACKWARD = [(i + 1, i) for i in range(TM - 1)]
INNER = [(i, i ^ 1) for i in range(SPACE)]
OUTER = [(i, ((i - 1) ^ 1) + 1 if 0 < i < SPACE - 1 else SPACE - 1 - i) for i in range(SPACE)]
SIBLING = [(i, i ^ 1) for i in range(TM)]


def edge_rows(table, *blocks, after=()):
    rows = shape((OWN * len(blocks), C, W), BF16)
    return call(edges_kernel, (rows, rows), (table, *blocks), after=after)


def row_halos(inner, outer):
    return lax.ppermute(inner, "space", INNER), lax.ppermute(outer, "space", OUTER)


SAME_CORE = [[(2 * x + core) * SPACE + s for x in range(CHIPS) for s in range(SPACE)] for core in range(2)]
SIDE = 4


def along(part, stride):
    near = [
        [(i, i - (i // stride % SIDE) * stride + ((i // stride + d) % SIDE) * stride) for i in range(SPACE)]
        for d in range(1, SIDE)
    ]
    return (part, *(lax.ppermute(part, "space", route) for route in near))


def shape(dims, dtype=F32):
    return jax.ShapeDtypeStruct(dims, dtype)


FIELD = (OWN, ROWS, C, W)
COLS = (6 * TAP_ROWS, 4 * W)


def shards(
    activations,
    weight_one,
    weight_two,
    gain_one,
    bias_one,
    gain_two,
    bias_two,
    cotangent,
    clip_lengths,
):
    table = pl.pallas_call(
        table_kernel,
        out_shape=shape((16, W)),
        in_specs=[pl.BlockSpec(memory_space=pltpu.SMEM)],
        out_specs=pl.BlockSpec(memory_space=pltpu.VMEM),
        compiler_params=pltpu.CompilerParams(vmem_limit_bytes=1024 * 1024),
    )(clip_lengths)
    params = jnp.stack([gain_one, bias_one, gain_two, bias_two], axis=1)
    turned_one, turned_two = weight_one.T, weight_two.T
    small = shape((8, W))
    turned = pltpu.VMEM((3, C, DEPTH), BF16)
    packed = shape((SPACE, HALF, W), BF16)
    dense = [pltpu.VMEM((ALL_TAPS, C), F32), pltpu.VMEM((3, OWN * ROWS * W, C), BF16)]

    previous = lax.ppermute(activations, "tm", FORWARD)
    following = lax.ppermute(cotangent, "tm", BACKWARD)
    part = call(stats_kernel, small, (activations, previous))
    parts_one = along(call(merge_kernel, small, along(part, 1)), SIDE)
    inner, outer = row_halos(*edge_rows(table, previous, activations, cotangent, following, after=(part,)))
    columns_one, conv_one, stats_one, part = call(
        conv_one_kernel,
        (shape(COLS, BF16), shape(FIELD), small, small),
        (table, *parts_one, activations, previous, inner, outer, params, turned_one),
        limit=12,
    )
    merged = call(merge_kernel, small, along(part, 1))
    parts_two = along(merged, SIDE)
    half_one = call(half_kernel, shape(FIELD, BF16), (conv_one,), after=(merged,))
    previous_two = lax.ppermute(half_one, "tm", FORWARD)
    grad_active_two = call(
        adjoint_two_kernel,
        shape(FIELD),
        (table, cotangent, following, inner, outer, turned_two),
        scratch=[pltpu.VMEM(COLS, BF16), turned],
        after=(merged,),
        limit=16,
    )
    grad_norm, stats_two, part = call(
        norm_two_kernel,
        (shape(FIELD), small, small),
        (*parts_two, conv_one, grad_active_two, params),
    )
    sums_two = along(call(sum_kernel, small, along(part, 1)), SIDE)
    earlier_two = lax.ppermute(stats_two, "tm", FORWARD)
    inner_two, outer_two = row_halos(*edge_rows(table, previous_two, half_one, after=(part,)))
    decoded, kept_two, sent_two, done_two = call(
        conv_two_kernel,
        (shape(FIELD, BF16), packed, packed, small),
        (
            table, stats_two, earlier_two, conv_one, previous_two, inner_two, outer_two, params, turned_two,
            activations, cotangent,
        ),
        scratch=[pltpu.VMEM(COLS, BF16)] + dense,
        after=(part,),
        limit=20,
    )
    came_two = lax.ppermute(sent_two, "tm", SIBLING)
    grad_conv_one = call(
        grad_conv_kernel, shape(FIELD, BF16), (stats_two, *sums_two, grad_norm, conv_one), after=(done_two,)
    )
    following_one = lax.ppermute(grad_conv_one, "tm", BACKWARD)
    kept_one, sent_one = call(
        weight_one_kernel, (packed, packed), (table, columns_one, grad_conv_one), scratch=dense, limit=16
    )
    came_one = lax.ppermute(sent_one, "tm", SIBLING)
    edges_one = edge_rows(table, grad_conv_one, following_one, after=(sent_one,))
    inner_one, outer_one = row_halos(*edges_one)
    pairs, done_pairs = call(
        pair_kernel,
        (shape((CHIPS * SPACE, 2 * PIECE, W), BF16), small),
        (kept_one, came_one, kept_two, came_two),
        after=(edges_one[0],),
    )
    swapped = lax.all_to_all(pairs, ("tm", "space"), 0, 0, axis_index_groups=SAME_CORE)
    grad_norm, part = call(
        adjoint_one_kernel,
        (shape(FIELD), small),
        (table, grad_conv_one, following_one, inner_one, outer_one, turned_one, stats_one, activations, params),
        scratch=[pltpu.VMEM(COLS, BF16), turned, pltpu.VMEM(FIELD, F32)],
        after=(done_pairs,),
        limit=16,
    )
    sums_one = along(call(sum_kernel, small, along(part, 1)), SIDE)
    input_grad = call(
        input_grad_kernel, shape(FIELD, BF16), (stats_one, *sums_one, grad_norm, activations, cotangent)
    )
    total_cells = OWN * TM * ROWS * SPACE * W
    spread = call(gather_kernel, shape((TM, 2 * PIECE, W), BF16), (swapped,), after=(part,))
    share_one, share_two = call(
        functools.partial(unpack_kernel, scale=float(total_cells) ** -0.5),
        (shape((C, SHARE)),) * 2,
        (lax.all_to_all(spread, "tm", 0, 0),),
    )
    return (decoded, input_grad, share_one.T, share_two.T)


def solution(mesh):
    placed = (
        P("tm", "space", None, None),
        P(),
        P(),
        P(),
        P(),
        P(),
        P(),
        P("tm", "space", None, None),
        P(),
    )
    return jax.shard_map(
        shards,
        mesh=mesh,
        in_specs=placed,
        out_specs=(
            P("tm", "space", None, None),
            P("tm", "space", None, None),
            P("space", None),
            P("space", None),
        ),
        check_vma=False,
    )
```

```python
import functools

import jax
import jax.numpy as jnp
from jax import lax
from jax.experimental import pallas as pl
from jax.experimental.pallas import tpu as pltpu
from jax.sharding import PartitionSpec as P

GROUPS = 32
NORM_EPSILON = 1e-05

C = 192
W = 128
PER_GROUP = C // GROUPS
ROWS = 4
OWN = 2
TAP_ROWS = 3 * C
DEPTH = 3 * TAP_ROWS
ALL_TAPS = 3 * DEPTH
SPACE = 16
TM = 8
CLIPS = 4
SHARE = ALL_TAPS // SPACE
PACKED = 512
HALF = PACKED // 2
CHIPS = TM // 2
PIECE = HALF // CHIPS
LOCAL_COUNT = ROWS * PER_GROUP * W
FULL_COUNT = LOCAL_COUNT * SPACE

F32 = jnp.float32
BF16 = jnp.bfloat16
EXACT = lax.Precision.HIGHEST


def call(kernel, out_shape, operands, scratch=(), after=(), limit=8):
    count, extra = len(operands), len(after)

    def body(*refs):
        kernel(*refs[:count], *refs[count + extra :])

    return pl.pallas_call(
        body,
        out_shape=out_shape,
        in_specs=[pl.BlockSpec(memory_space=pltpu.VMEM)] * count + [pl.BlockSpec(memory_space=pl.ANY)] * extra,
        out_specs=jax.tree.map(lambda _: pl.BlockSpec(memory_space=pltpu.VMEM), out_shape),
        scratch_shapes=list(scratch),
        compiler_params=pltpu.CompilerParams(vmem_limit_bytes=limit * 1024 * 1024),
        cost_estimate=pl.CostEstimate(flops=0, bytes_accessed=0, transcendentals=0),
    )(*operands, *after)


def lane_ids(rows=C):
    return lax.broadcasted_iota(jnp.int32, (rows, W), 1)


def membership():
    channel = lax.broadcasted_iota(jnp.int32, (C, W), 0)
    group = lane_ids()
    inside = (channel >= group * PER_GROUP) & (channel < (group + 1) * PER_GROUP)
    return inside.astype(F32)


def to_groups(columns):
    lanes = lane_ids()
    packed = jnp.zeros((C, W), F32)
    for i, column in enumerate(columns):
        packed = jnp.where(lanes == i, column, packed)
    summed = lax.dot_general(
        packed, membership(), (((0,), (0,)), ((), ())), precision=EXACT, preferred_element_type=F32
    )
    return summed[:8]


def to_channels(table):
    return lax.dot_general(
        membership(), table, (((1,), (1,)), ((), ())), precision=EXACT, preferred_element_type=F32
    )


def merge(parts, count):
    mean = sum(part[0:4] for part in parts) * (1.0 / len(parts))
    spread = sum((part[0:4] - mean) ** 2 for part in parts) * float(count)
    return mean, sum(part[4:8] for part in parts) + spread


def stats_table(mean, squares):
    return jnp.concatenate([mean, lax.rsqrt(squares * (1.0 / FULL_COUNT) + NORM_EPSILON)], axis=0)


def local_stats(blocks):
    sums = []
    for rows in blocks:
        total = rows[0]()
        for row in rows[1:]:
            total = total + row()
        sums.append(jnp.sum(total, axis=1, keepdims=True))
    means = to_groups(sums) * (1.0 / LOCAL_COUNT)
    spread = to_channels(means)
    squares = []
    for f, rows in enumerate(blocks):
        total = None
        for row in rows:
            centered = row() - spread[:, f : f + 1]
            total = centered * centered if total is None else total + centered * centered
        squares.append(jnp.sum(total, axis=1, keepdims=True))
    deviations = to_groups(squares)
    return jnp.concatenate([means[:4], deviations[:4]], axis=0)


def store_shifted(cols_ref, h, f, field):
    lanes = lane_ids()
    before = jnp.where(lanes == 0, 0.0, pltpu.roll(field, 1, 1))
    after = jnp.where(lanes == W - 1, 0.0, pltpu.roll(field, W - 1, 1))
    for s, part in enumerate((before, field, after)):
        start = h * TAP_ROWS + s * C
        cols_ref[start : start + C, f * W : (f + 1) * W] = part.astype(BF16)


def conv_rows(kernels, cols_ref, factors, finish):
    for h in range(ROWS):
        total = None
        for k in range(3):
            part = jnp.dot(
                kernels[k],
                cols_ref[h * TAP_ROWS : h * TAP_ROWS + DEPTH, k * W : (k + 2) * W],
                preferred_element_type=F32,
            )
            if factors[k] is not None:
                part = part * factors[k]
            total = part if total is None else total + part
        finish(h, total)


def factor(table_ref, lag, frame):
    at = lag * 4 + frame
    return jnp.concatenate([table_ref[at : at + 1, :], table_ref[at + 1 : at + 2, :]], axis=1)


def edges_kernel(table_ref, *refs):
    odd = jnp.broadcast_to(table_ref[15:16, :], (C, W)) > 0.5
    inner_ref, outer_ref = refs[-2:]
    for i, ref in enumerate(refs[:-2]):
        for f in range(OWN):
            low, high = ref[f, ROWS - 1].astype(F32), ref[f, 0].astype(F32)
            inner_ref[i * OWN + f] = jnp.where(odd, high, low).astype(BF16)
            outer_ref[i * OWN + f] = jnp.where(odd, low, high).astype(BF16)


def beside(table_ref, inner_ref, outer_ref, i):
    odd = jnp.broadcast_to(table_ref[15:16, :], (C, W)) > 0.5
    inner, outer = inner_ref[i].astype(F32), outer_ref[i].astype(F32)
    above = jnp.where(odd, inner, outer) * table_ref[12:13, :]
    below = jnp.where(odd, outer, inner) * table_ref[13:14, :]
    return above, below


def stats_kernel(own_ref, copy_ref, out_ref):
    def row(f, h):
        return lambda: own_ref[f, h].astype(F32)

    out_ref[...] = local_stats([[row(f, h) for h in range(ROWS)] for f in range(OWN)])
    copy_ref[...] = own_ref[...]


def join_kernel(prev_ref, own_ref, cot_ref, out_ref, copy_ref):
    for i, ref in enumerate((prev_ref, own_ref)):
        out_ref[i * OWN : (i + 1) * OWN] = ref[0:OWN]
        out_ref[4 + i * OWN : 4 + (i + 1) * OWN] = ref[4 : 4 + OWN]
    copy_ref[...] = cot_ref[...]


def silu_of(pre):
    return pre / (1.0 + jnp.exp(-pre))


def active_columns(cols_ref, table_ref, stats, gain, bias, own, prev, inner, outer):
    shift = jnp.broadcast_to(bias, (C, W))
    for f in range(4):
        mean = jnp.broadcast_to(stats[f][0], (C, W))
        scale = jnp.broadcast_to(stats[f][1] * gain, (C, W))
        ends = beside(table_ref, inner, outer, f)
        for h in range(ROWS + 2):
            if h == 0:
                field = ends[0]
            elif h == ROWS + 1:
                field = ends[1]
            else:
                field = (prev if f < OWN else own)[f % OWN, h - 1].astype(F32)
            active = silu_of((field - mean) * scale + shift)
            if h == 0:
                active = active * table_ref[12:13, :]
            if h == ROWS + 1:
                active = active * table_ref[13:14, :]
            store_shifted(cols_ref, h, f, active)


def forward_conv(table_ref, weight_ref, cols_ref, finish):
    kernels = [weight_ref[:, k * DEPTH : (k + 1) * DEPTH] for k in range(3)]
    factors = [factor(table_ref, 2 - k, 0) for k in range(2)] + [None]
    conv_rows(kernels, cols_ref, factors, finish)


def conv_one_kernel(
    table_ref, part_ref, a_ref, b_ref, c_ref, own_ref, prev_ref, inner_ref, outer_ref, param_ref, weight_ref,
    cols_ref, conv_ref, stats_ref, out_ref,
):
    parts = [ref[...] for ref in (part_ref, a_ref, b_ref, c_ref)]
    merged = stats_table(*merge(parts, 4 * LOCAL_COUNT))
    stats_ref[...] = merged
    wide = to_channels(merged)
    stats = [(wide[:, f : f + 1], wide[:, 4 + f : 5 + f]) for f in range(4)]
    active_columns(
        cols_ref, table_ref, stats, param_ref[:, 0:1], param_ref[:, 1:2], own_ref, prev_ref, inner_ref, outer_ref
    )

    def finish(h, total):
        for f in range(OWN):
            conv_ref[f, h] = total[:, f * W : (f + 1) * W]

    forward_conv(table_ref, weight_ref, cols_ref, finish)

    def row(f, h):
        return lambda: conv_ref[f, h]

    out_ref[...] = local_stats([[row(f, h) for h in range(ROWS)] for f in range(OWN)])


def merge_kernel(own_ref, a_ref, b_ref, c_ref, out_ref):
    mean, squares = merge([ref[...] for ref in (own_ref, a_ref, b_ref, c_ref)], LOCAL_COUNT)
    out_ref[...] = jnp.concatenate([mean, squares], axis=0)


def sum_kernel(own_ref, a_ref, b_ref, c_ref, out_ref):
    out_ref[...] = own_ref[...] + a_ref[...] + b_ref[...] + c_ref[...]


def turn(src_ref, dst_ref):
    row = lax.broadcasted_iota(jnp.int32, (C, C), 0)
    eye = (row == lax.broadcasted_iota(jnp.int32, (C, C), 1)).astype(BF16)
    for tap in range(27):
        k, spot = divmod(26 - tap, 9)
        block = lax.dot_general(
            eye, src_ref[:, tap * C : (tap + 1) * C], (((1,), (1,)), ((), ())), preferred_element_type=F32
        )
        dst_ref[k, :, spot * C : (spot + 1) * C] = block.astype(BF16)


def adjoint(table_ref, own_ref, next_ref, inner_ref, outer_ref, weight_ref, out_ref, cols_ref, turned_ref, first):
    for f in range(4):
        ends = beside(table_ref, inner_ref, outer_ref, first + f)
        for h in range(ROWS + 2):
            if h == 0:
                field = ends[0]
            elif h == ROWS + 1:
                field = ends[1]
            else:
                field = (own_ref if f < OWN else next_ref)[f % OWN, h - 1].astype(F32)
            store_shifted(cols_ref, h, f, field)
    turn(weight_ref, turned_ref)
    factors = [None] + [factor(table_ref, j, j) for j in (1, 2)]

    def finish(h, total):
        out_ref[0, h] = total[:, :W]
        out_ref[1, h] = total[:, W:]

    conv_rows([turned_ref[j] for j in range(3)], cols_ref, factors, finish)


def adjoint_two_kernel(
    table_ref, own_ref, next_ref, inner_ref, outer_ref, weight_ref, out_ref, cols_ref, turned_ref
):
    adjoint(table_ref, own_ref, next_ref, inner_ref, outer_ref, weight_ref, out_ref, cols_ref, turned_ref, 4)


def adjoint_one_kernel(
    table_ref, own_ref, next_ref, inner_ref, outer_ref, weight_ref, stats_ref, field_ref, param_ref,
    grad_ref, out_ref, cols_ref, turned_ref, upstream_ref,
):
    adjoint(
        table_ref, own_ref, next_ref, inner_ref, outer_ref, weight_ref, upstream_ref, cols_ref, turned_ref, 0
    )
    wide = to_channels(stats_ref[...])
    stats = [(wide[:, 2 + f : 3 + f], wide[:, 6 + f : 7 + f]) for f in range(OWN)]
    out_ref[...] = norm_grad(stats, field_ref, upstream_ref, param_ref, grad_ref, 0)


def norm_grad(stats, field_ref, upstream_ref, param_ref, grad_ref, place, active_ref=None):
    gain = jnp.broadcast_to(param_ref[:, place : place + 1], (C, W))
    bias = jnp.broadcast_to(param_ref[:, place + 1 : place + 2], (C, W))
    plain, weighted = [], []
    for f in range(OWN):
        mean = jnp.broadcast_to(stats[f][0], (C, W))
        inverse = jnp.broadcast_to(stats[f][1], (C, W))
        sums = None
        for h in range(ROWS):
            normalized = (field_ref[f, h].astype(F32) - mean) * inverse
            pre = normalized * gain + bias
            sigmoid = 1.0 / (1.0 + jnp.exp(-pre))
            grad = upstream_ref[f, h] * (sigmoid * (1.0 + pre * (1.0 - sigmoid))) * gain
            grad_ref[f, h] = grad
            if active_ref is not None:
                active_ref[f, h] = (pre * sigmoid).astype(BF16)
            pair = (grad, grad * normalized)
            sums = pair if sums is None else (sums[0] + pair[0], sums[1] + pair[1])
        plain.append(jnp.sum(sums[0], axis=1, keepdims=True))
        weighted.append(jnp.sum(sums[1], axis=1, keepdims=True))
    return to_groups(plain + weighted)


def norm_two_kernel(
    own_ref, a_ref, b_ref, c_ref, field_ref, upstream_ref, param_ref, active_ref, grad_ref, stats_ref, out_ref
):
    parts = [ref[...] for ref in (own_ref, a_ref, b_ref, c_ref)]
    merged = stats_table(*merge(parts, 4 * LOCAL_COUNT))
    stats_ref[...] = merged
    wide = to_channels(merged)
    stats = [(wide[:, f : f + 1], wide[:, 4 + f : 5 + f]) for f in range(OWN)]
    out_ref[...] = norm_grad(stats, field_ref, upstream_ref, param_ref, grad_ref, 2, active_ref)


def field_grad(stats, sums, grad_ref, field_ref, finish):
    totals = to_channels(sums * (1.0 / FULL_COUNT))
    for f in range(OWN):
        mean = jnp.broadcast_to(stats[f][0], (C, W))
        inverse = jnp.broadcast_to(stats[f][1], (C, W))
        plain = jnp.broadcast_to(totals[:, f : f + 1], (C, W))
        weighted = jnp.broadcast_to(totals[:, OWN + f : OWN + f + 1], (C, W))
        for h in range(ROWS):
            normalized = (field_ref[f, h].astype(F32) - mean) * inverse
            finish(f, h, inverse * (grad_ref[f, h] - plain - normalized * weighted))


def grad_conv_kernel(stats_ref, own_ref, a_ref, b_ref, c_ref, grad_ref, field_ref, out_ref):
    def finish(f, h, value):
        out_ref[f, h] = value.astype(BF16)

    wide = to_channels(stats_ref[...])
    stats = [(wide[:, f : f + 1], wide[:, 4 + f : 5 + f]) for f in range(OWN)]
    field_grad(stats, own_ref[...] + a_ref[...] + b_ref[...] + c_ref[...], grad_ref, field_ref, finish)


def input_grad_kernel(stats_ref, own_ref, a_ref, b_ref, c_ref, grad_ref, field_ref, cot_ref, out_ref):
    def finish(f, h, value):
        out_ref[f, h] = (cot_ref[f, h].astype(F32) + value).astype(BF16)

    wide = to_channels(stats_ref[...])
    stats = [(wide[:, 2 + f : 3 + f], wide[:, 6 + f : 7 + f]) for f in range(OWN)]
    field_grad(stats, own_ref[...] + a_ref[...] + b_ref[...] + c_ref[...], grad_ref, field_ref, finish)


def weight_kernel(table_ref, cols_ref, grad_ref, kept_ref, send_ref, dense_ref, turned_ref):
    for h in range(ROWS):
        for f in range(OWN):
            block = grad_ref[f, h].T
            start = (h * OWN + f) * W
            turned_ref[2, start : start + W, :] = block
            wide = block.astype(F32)
            for k in range(2):
                at = (2 - k) * 4 + f
                turned_ref[k, start : start + W, :] = (wide * table_ref[at : at + 1, 0:1]).astype(BF16)
    for k in range(3):
        for spot in range(9):
            start = spot * C
            rows = [
                cols_ref[h * TAP_ROWS + start : h * TAP_ROWS + start + C, k * W : (k + 2) * W]
                for h in range(ROWS)
            ]
            dense_ref[k * DEPTH + start : k * DEPTH + start + C, :] = jnp.dot(
                jnp.concatenate(rows, axis=1), turned_ref[k], preferred_element_type=F32
            )
    half = SHARE // 2
    first = jnp.broadcast_to(table_ref[14:15, :], (HALF, W)) < 0.5
    for s in range(SPACE):
        low = dense_ref[s * SHARE : (s + 1) * SHARE, 0:W]
        high = jnp.concatenate(
            [
                dense_ref[s * SHARE : s * SHARE + half, W:C],
                dense_ref[s * SHARE + half : (s + 1) * SHARE, W:C],
            ],
            axis=1,
        )
        spare = jnp.zeros((PACKED - SHARE - half, W), F32)
        packed = jnp.concatenate([low, high, spare], axis=0).astype(BF16)
        kept_ref[s] = jnp.where(first, packed[:HALF], packed[HALF:])
        send_ref[s] = jnp.where(first, packed[HALF:], packed[:HALF])


def conv_two_kernel(
    table_ref, own_ref, prev_ref, inner_ref, outer_ref, weight_ref, input_ref, decoded_ref, cols_ref
):
    for f in range(4):
        ends = beside(table_ref, inner_ref, outer_ref, f)
        for h in range(ROWS + 2):
            if h == 0:
                field = ends[0]
            elif h == ROWS + 1:
                field = ends[1]
            else:
                field = (prev_ref if f < OWN else own_ref)[f % OWN, h - 1].astype(F32)
            store_shifted(cols_ref, h, f, field)

    def finish(h, total):
        for f in range(OWN):
            field = input_ref[f, h].astype(F32) + total[:, f * W : (f + 1) * W]
            decoded_ref[f, h] = field.astype(BF16)

    forward_conv(table_ref, weight_ref, cols_ref, finish)


def pair_kernel(kept_one_ref, came_one_ref, kept_two_ref, came_two_ref, out_ref, done_ref):
    for i, (kept, came) in enumerate(((kept_one_ref, came_one_ref), (kept_two_ref, came_two_ref))):
        for x in range(CHIPS):
            rows = slice(x * PIECE, (x + 1) * PIECE)
            total = kept[:, rows].astype(F32) + came[:, rows].astype(F32)
            out_ref[x * SPACE : (x + 1) * SPACE, i * PIECE : (i + 1) * PIECE] = total.astype(BF16)
    done_ref[...] = jnp.zeros((8, W), F32)


def gather_kernel(parts_ref, out_ref):
    total = parts_ref[0].astype(F32)
    for s in range(1, CHIPS * SPACE):
        total = total + parts_ref[s].astype(F32)
    total = total.astype(BF16)
    for i in range(TM):
        out_ref[i] = total


def unpack_kernel(parts_ref, one_ref, two_ref, *, scale):
    half = SHARE // 2
    for i, out_ref in enumerate((one_ref, two_ref)):
        pieces = [
            parts_ref[2 * x + core, i * PIECE : (i + 1) * PIECE].astype(F32)
            for core in range(2)
            for x in range(CHIPS)
        ]
        packed = jnp.concatenate(pieces, axis=0) * scale
        high = packed[SHARE : SHARE + half]
        out_ref[0:W, :] = packed[0:SHARE].T
        out_ref[W:C, 0:half] = high[:, : C - W].T
        out_ref[W:C, half:SHARE] = high[:, C - W :].T


def table_kernel(lengths_ref, out_ref):
    place, row = lax.axis_index("tm"), lax.axis_index("space")
    ends, end = [], 0
    for i in range(CLIPS):
        end = end + lengths_ref[i]
        ends.append(end)

    def clip_of(frame):
        return sum((frame >= end).astype(jnp.int32) for end in ends)

    values = []
    for lag in range(3):
        for f in range(4):
            frame = place * OWN + f
            kept = (frame >= lag) & (clip_of(frame - lag) == clip_of(frame))
            values.append(kept.astype(F32) if lag else jnp.float32(1.0))
    flags = (row > 0, row < SPACE - 1, place % 2 > 0, row % 2 > 0)
    for i, value in enumerate(values + [flag.astype(F32) for flag in flags]):
        out_ref[i : i + 1, :] = jnp.full((1, W), value, F32)


FORWARD = [(i, i + 1) for i in range(TM - 1)]
BACKWARD = [(i + 1, i) for i in range(TM - 1)]
INNER = [(i, i ^ 1) for i in range(SPACE)]
OUTER = [(i, ((i - 1) ^ 1) + 1 if 0 < i < SPACE - 1 else SPACE - 1 - i) for i in range(SPACE)]
SIBLING = [(i, i ^ 1) for i in range(TM)]


def edge_rows(table, *blocks, after=()):
    rows = shape((OWN * len(blocks), C, W), BF16)
    return call(edges_kernel, (rows, rows), (table, *blocks), after=after)


def row_halos(inner, outer):
    return lax.ppermute(inner, "space", INNER), lax.ppermute(outer, "space", OUTER)


SAME_CORE = [[(2 * x + core) * SPACE + s for x in range(CHIPS) for s in range(SPACE)] for core in range(2)]
SIDE = 4


def along(part, stride):
    near = [
        [(i, i - (i // stride % SIDE) * stride + ((i // stride + d) % SIDE) * stride) for i in range(SPACE)]
        for d in range(1, SIDE)
    ]
    return (part, *(lax.ppermute(part, "space", route) for route in near))


def shape(dims, dtype=F32):
    return jax.ShapeDtypeStruct(dims, dtype)


FIELD = (OWN, ROWS, C, W)
COLS = (6 * TAP_ROWS, 4 * W)


def shards(
    activations,
    weight_one,
    weight_two,
    gain_one,
    bias_one,
    gain_two,
    bias_two,
    cotangent,
    clip_lengths,
):
    table = pl.pallas_call(
        table_kernel,
        out_shape=shape((16, W)),
        in_specs=[pl.BlockSpec(memory_space=pltpu.SMEM)],
        out_specs=pl.BlockSpec(memory_space=pltpu.VMEM),
        compiler_params=pltpu.CompilerParams(vmem_limit_bytes=1024 * 1024),
    )(clip_lengths)
    params = jnp.stack([gain_one, bias_one, gain_two, bias_two], axis=1)
    turned_one, turned_two = weight_one.T, weight_two.T
    small = shape((8, W))
    turned = pltpu.VMEM((3, C, DEPTH), BF16)
    packed = shape((SPACE, HALF, W), BF16)
    dense = [pltpu.VMEM((ALL_TAPS, C), F32), pltpu.VMEM((3, OWN * ROWS * W, C), BF16)]

    fields, part = call(stats_kernel, (shape(FIELD, BF16), small), (activations,))
    part, upstream = call(
        join_kernel, (small, shape(FIELD, BF16)), (lax.ppermute(part, "tm", FORWARD), part, cotangent)
    )
    previous = lax.ppermute(fields, "tm", FORWARD)
    following = lax.ppermute(upstream, "tm", BACKWARD)
    merged = call(merge_kernel, small, along(part, 1))
    parts_one = along(merged, SIDE)
    inner, outer = row_halos(*edge_rows(table, previous, fields, upstream, following, after=(merged,)))
    columns_one, conv_one, stats_one, part = call(
        conv_one_kernel,
        (shape(COLS, BF16), shape(FIELD), small, small),
        (table, *parts_one, fields, previous, inner, outer, params, turned_one),
        limit=12,
    )
    merged = call(merge_kernel, small, along(part, 1))
    parts_two = along(merged, SIDE)
    grad_active_two = call(
        adjoint_two_kernel,
        shape(FIELD),
        (table, upstream, following, inner, outer, turned_two),
        scratch=[pltpu.VMEM(COLS, BF16), turned],
        after=(merged,),
        limit=16,
    )
    active_two, grad_norm, stats_two, part = call(
        norm_two_kernel,
        (shape(FIELD, BF16), shape(FIELD), small, small),
        (*parts_two, conv_one, grad_active_two, params),
    )
    merged = call(sum_kernel, small, along(part, 1))
    sums_two = along(merged, SIDE)
    previous_two = lax.ppermute(active_two, "tm", FORWARD)
    inner_two, outer_two = row_halos(*edge_rows(table, previous_two, active_two, after=(merged,)))
    decoded, columns_two = call(
        conv_two_kernel,
        (shape(FIELD, BF16), shape(COLS, BF16)),
        (table, active_two, previous_two, inner_two, outer_two, turned_two, fields),
        limit=12,
    )
    grad_conv_one = call(
        grad_conv_kernel, shape(FIELD, BF16), (stats_two, *sums_two, grad_norm, conv_one), after=(columns_two,)
    )
    following_one = lax.ppermute(grad_conv_one, "tm", BACKWARD)
    kept_two, sent_two = call(
        weight_kernel,
        (packed, packed),
        (table, columns_two, upstream),
        scratch=dense,
        after=(grad_conv_one,),
        limit=16,
    )
    came_two = lax.ppermute(sent_two, "tm", SIBLING)
    edges_one = edge_rows(table, grad_conv_one, following_one, after=(sent_two,))
    inner_one, outer_one = row_halos(*edges_one)
    kept_one, sent_one = call(
        weight_kernel,
        (packed, packed),
        (table, columns_one, grad_conv_one),
        scratch=dense,
        after=(edges_one[0],),
        limit=16,
    )
    came_one = lax.ppermute(sent_one, "tm", SIBLING)
    pairs, done_pairs = call(
        pair_kernel,
        (shape((CHIPS * SPACE, 2 * PIECE, W), BF16), small),
        (kept_one, came_one, kept_two, came_two),
        after=(inner_one, outer_one),
    )
    swapped = lax.all_to_all(pairs, ("tm", "space"), 0, 0, axis_index_groups=SAME_CORE)
    grad_norm, part = call(
        adjoint_one_kernel,
        (shape(FIELD), small),
        (table, grad_conv_one, following_one, inner_one, outer_one, turned_one, stats_one, fields, params),
        scratch=[pltpu.VMEM(COLS, BF16), turned, pltpu.VMEM(FIELD, F32)],
        after=(done_pairs,),
        limit=16,
    )
    merged = call(sum_kernel, small, along(part, 1))
    sums_one = along(merged, SIDE)
    input_grad = call(
        input_grad_kernel, shape(FIELD, BF16), (stats_one, *sums_one, grad_norm, fields, upstream)
    )
    total_cells = OWN * TM * ROWS * SPACE * W
    spread = call(gather_kernel, shape((TM, 2 * PIECE, W), BF16), (swapped,), after=(merged,))
    share_one, share_two = call(
        functools.partial(unpack_kernel, scale=float(total_cells) ** -0.5),
        (shape((C, SHARE)),) * 2,
        (lax.all_to_all(spread, "tm", 0, 0),),
    )
    return (decoded, input_grad, share_one.T, share_two.T)


def solution(mesh):
    placed = (
        P("tm", "space", None, None),
        P(),
        P(),
        P(),
        P(),
        P(),
        P(),
        P("tm", "space", None, None),
        P(),
    )
    return jax.shard_map(
        shards,
        mesh=mesh,
        in_specs=placed,
        out_specs=(
            P("tm", "space", None, None),
            P("tm", "space", None, None),
            P("space", None),
            P("space", None),
        ),
        check_vma=False,
    )
```

```python
import functools

import jax
import jax.numpy as jnp
from jax import lax
from jax.experimental import pallas as pl
from jax.experimental.pallas import tpu as pltpu
from jax.sharding import PartitionSpec as P

GROUPS = 32
NORM_EPSILON = 1e-05

C = 192
W = 128
PER_GROUP = C // GROUPS
ROWS = 4
OWN = 2
TAP_ROWS = 3 * C
DEPTH = 3 * TAP_ROWS
ALL_TAPS = 3 * DEPTH
SPACE = 16
TM = 8
CLIPS = 4
SHARE = ALL_TAPS // SPACE
PACKED = 512
HALF = PACKED // 2
CHIPS = TM // 2
LOCAL_COUNT = ROWS * PER_GROUP * W
FULL_COUNT = LOCAL_COUNT * SPACE

F32 = jnp.float32
BF16 = jnp.bfloat16
EXACT = lax.Precision.HIGHEST


def call(kernel, out_shape, operands, scratch=(), after=(), limit=8, smem=0):
    count, extra = len(operands), len(after)

    def body(*refs):
        kernel(*refs[:count], *refs[count + extra :])

    return pl.pallas_call(
        body,
        out_shape=out_shape,
        in_specs=[pl.BlockSpec(memory_space=pltpu.SMEM)] * smem
        + [pl.BlockSpec(memory_space=pltpu.VMEM)] * (count - smem)
        + [pl.BlockSpec(memory_space=pl.ANY)] * extra,
        out_specs=jax.tree.map(lambda _: pl.BlockSpec(memory_space=pltpu.VMEM), out_shape),
        scratch_shapes=list(scratch),
        compiler_params=pltpu.CompilerParams(vmem_limit_bytes=limit * 1024 * 1024),
        cost_estimate=pl.CostEstimate(flops=0, bytes_accessed=0, transcendentals=0),
    )(*operands, *after)


def lane_ids(rows=C):
    return lax.broadcasted_iota(jnp.int32, (rows, W), 1)


def membership():
    channel = lax.broadcasted_iota(jnp.int32, (C, W), 0)
    group = lane_ids()
    inside = (channel >= group * PER_GROUP) & (channel < (group + 1) * PER_GROUP)
    return inside.astype(F32)


def to_groups(columns):
    lanes = lane_ids()
    packed = jnp.zeros((C, W), F32)
    for i, column in enumerate(columns):
        packed = jnp.where(lanes == i, column, packed)
    summed = lax.dot_general(
        packed, membership(), (((0,), (0,)), ((), ())), precision=EXACT, preferred_element_type=F32
    )
    return summed[:8]


def to_channels(table):
    return lax.dot_general(
        membership(), table, (((1,), (1,)), ((), ())), precision=EXACT, preferred_element_type=F32
    )


def merge(parts, count):
    mean = sum(part[0:4] for part in parts) * (1.0 / len(parts))
    spread = sum((part[0:4] - mean) ** 2 for part in parts) * float(count)
    return mean, sum(part[4:8] for part in parts) + spread


def stats_table(mean, squares):
    return jnp.concatenate([mean, lax.rsqrt(squares * (1.0 / FULL_COUNT) + NORM_EPSILON)], axis=0)


def local_stats(blocks):
    sums = []
    for rows in blocks:
        total = rows[0]()
        for row in rows[1:]:
            total = total + row()
        sums.append(jnp.sum(total, axis=1, keepdims=True))
    means = to_groups(sums) * (1.0 / LOCAL_COUNT)
    spread = to_channels(means)
    squares = []
    for f, rows in enumerate(blocks):
        total = None
        for row in rows:
            centered = row() - spread[:, f : f + 1]
            total = centered * centered if total is None else total + centered * centered
        squares.append(jnp.sum(total, axis=1, keepdims=True))
    deviations = to_groups(squares)
    return jnp.concatenate([means[:4], deviations[:4]], axis=0)


def store_shifted(cols_ref, h, f, field):
    lanes = lane_ids()
    before = jnp.where(lanes == 0, 0.0, pltpu.roll(field, 1, 1))
    after = jnp.where(lanes == W - 1, 0.0, pltpu.roll(field, W - 1, 1))
    for s, part in enumerate((before, field, after)):
        start = h * TAP_ROWS + s * C
        cols_ref[start : start + C, f * W : (f + 1) * W] = part.astype(BF16)


def conv_rows(kernels, cols_ref, factors, finish):
    for h in range(ROWS):
        total = None
        for k in range(3):
            part = jnp.dot(
                kernels[k],
                cols_ref[h * TAP_ROWS : h * TAP_ROWS + DEPTH, k * W : (k + 2) * W],
                preferred_element_type=F32,
            )
            if factors[k] is not None:
                part = part * factors[k]
            total = part if total is None else total + part
        finish(h, total)


def factor(table_ref, lag, frame):
    at = lag * 4 + frame
    return jnp.concatenate([table_ref[at : at + 1, :], table_ref[at + 1 : at + 2, :]], axis=1)


def edges_kernel(table_ref, *refs):
    odd = jnp.broadcast_to(table_ref[15:16, :], (C, W)) > 0.5
    inner_ref, outer_ref = refs[-2:]
    for i, ref in enumerate(refs[:-2]):
        for f in range(OWN):
            low, high = ref[f, ROWS - 1].astype(F32), ref[f, 0].astype(F32)
            inner_ref[i * OWN + f] = jnp.where(odd, high, low).astype(BF16)
            outer_ref[i * OWN + f] = jnp.where(odd, low, high).astype(BF16)


def beside(table_ref, inner_ref, outer_ref, i):
    odd = jnp.broadcast_to(table_ref[15:16, :], (C, W)) > 0.5
    inner, outer = inner_ref[i].astype(F32), outer_ref[i].astype(F32)
    above = jnp.where(odd, inner, outer) * table_ref[12:13, :]
    below = jnp.where(odd, outer, inner) * table_ref[13:14, :]
    return above, below


def stats_kernel(own_ref, copy_ref, out_ref):
    def row(f, h):
        return lambda: own_ref[f, h].astype(F32)

    out_ref[...] = local_stats([[row(f, h) for h in range(ROWS)] for f in range(OWN)])
    copy_ref[...] = own_ref[...]


def copy_kernel(src_ref, out_ref):
    out_ref[...] = src_ref[...]


def join_kernel(prev_ref, own_ref, cot_ref, out_ref, copy_ref):
    for i, ref in enumerate((prev_ref, own_ref)):
        out_ref[i * OWN : (i + 1) * OWN] = ref[0:OWN]
        out_ref[4 + i * OWN : 4 + (i + 1) * OWN] = ref[4 : 4 + OWN]
    copy_ref[...] = cot_ref[...]


def silu_of(pre):
    return pre / (1.0 + jnp.exp(-pre))


def active_columns(cols_ref, table_ref, stats, gain, bias, own, prev, inner, outer):
    shift = jnp.broadcast_to(bias, (C, W))
    for f in range(4):
        mean = jnp.broadcast_to(stats[f][0], (C, W))
        scale = jnp.broadcast_to(stats[f][1] * gain, (C, W))
        ends = beside(table_ref, inner, outer, f)
        for h in range(ROWS + 2):
            if h == 0:
                field = ends[0]
            elif h == ROWS + 1:
                field = ends[1]
            else:
                field = (prev if f < OWN else own)[f % OWN, h - 1].astype(F32)
            active = silu_of((field - mean) * scale + shift)
            if h == 0:
                active = active * table_ref[12:13, :]
            if h == ROWS + 1:
                active = active * table_ref[13:14, :]
            store_shifted(cols_ref, h, f, active)


def forward_conv(table_ref, weight_ref, cols_ref, finish):
    kernels = [weight_ref[:, k * DEPTH : (k + 1) * DEPTH] for k in range(3)]
    factors = [factor(table_ref, 2 - k, 0) for k in range(2)] + [None]
    conv_rows(kernels, cols_ref, factors, finish)


def conv_one_kernel(
    table_ref, part_ref, a_ref, b_ref, c_ref, own_ref, prev_ref, inner_ref, outer_ref, param_ref, weight_ref,
    cols_ref, conv_ref, stats_ref, out_ref,
):
    parts = [ref[...] for ref in (part_ref, a_ref, b_ref, c_ref)]
    merged = stats_table(*merge(parts, 4 * LOCAL_COUNT))
    stats_ref[...] = merged
    wide = to_channels(merged)
    stats = [(wide[:, f : f + 1], wide[:, 4 + f : 5 + f]) for f in range(4)]
    active_columns(
        cols_ref, table_ref, stats, param_ref[:, 0:1], param_ref[:, 1:2], own_ref, prev_ref, inner_ref, outer_ref
    )

    def finish(h, total):
        for f in range(OWN):
            conv_ref[f, h] = total[:, f * W : (f + 1) * W]

    forward_conv(table_ref, weight_ref, cols_ref, finish)

    def row(f, h):
        return lambda: conv_ref[f, h]

    out_ref[...] = local_stats([[row(f, h) for h in range(ROWS)] for f in range(OWN)])


def merge_kernel(own_ref, a_ref, b_ref, c_ref, out_ref):
    mean, squares = merge([ref[...] for ref in (own_ref, a_ref, b_ref, c_ref)], LOCAL_COUNT)
    out_ref[...] = jnp.concatenate([mean, squares], axis=0)


def sum_kernel(own_ref, a_ref, b_ref, c_ref, out_ref):
    out_ref[...] = own_ref[...] + a_ref[...] + b_ref[...] + c_ref[...]


def turn(src_ref, dst_ref):
    row = lax.broadcasted_iota(jnp.int32, (C, C), 0)
    eye = (row == lax.broadcasted_iota(jnp.int32, (C, C), 1)).astype(BF16)
    for tap in range(27):
        k, spot = divmod(26 - tap, 9)
        block = lax.dot_general(
            eye, src_ref[:, tap * C : (tap + 1) * C], (((1,), (1,)), ((), ())), preferred_element_type=F32
        )
        dst_ref[k, :, spot * C : (spot + 1) * C] = block.astype(BF16)


def adjoint(table_ref, own_ref, next_ref, inner_ref, outer_ref, weight_ref, out_ref, cols_ref, turned_ref, first):
    for f in range(4):
        ends = beside(table_ref, inner_ref, outer_ref, first + f)
        for h in range(ROWS + 2):
            if h == 0:
                field = ends[0]
            elif h == ROWS + 1:
                field = ends[1]
            else:
                field = (own_ref if f < OWN else next_ref)[f % OWN, h - 1].astype(F32)
            store_shifted(cols_ref, h, f, field)
    turn(weight_ref, turned_ref)
    factors = [None] + [factor(table_ref, j, j) for j in (1, 2)]

    def finish(h, total):
        out_ref[0, h] = total[:, :W]
        out_ref[1, h] = total[:, W:]

    conv_rows([turned_ref[j] for j in range(3)], cols_ref, factors, finish)


def adjoint_two_kernel(
    table_ref, own_ref, next_ref, inner_ref, outer_ref, weight_ref, out_ref, cols_ref, turned_ref
):
    adjoint(table_ref, own_ref, next_ref, inner_ref, outer_ref, weight_ref, out_ref, cols_ref, turned_ref, 4)


def adjoint_one_kernel(
    table_ref, own_ref, next_ref, inner_ref, outer_ref, weight_ref, stats_ref, field_ref, param_ref,
    grad_ref, out_ref, cols_ref, turned_ref, upstream_ref,
):
    adjoint(
        table_ref, own_ref, next_ref, inner_ref, outer_ref, weight_ref, upstream_ref, cols_ref, turned_ref, 0
    )
    wide = to_channels(stats_ref[...])
    stats = [(wide[:, 2 + f : 3 + f], wide[:, 6 + f : 7 + f]) for f in range(OWN)]
    out_ref[...] = norm_grad(stats, field_ref, upstream_ref, param_ref, grad_ref, 0)


def norm_grad(stats, field_ref, upstream_ref, param_ref, grad_ref, place, active_ref=None):
    gain = jnp.broadcast_to(param_ref[:, place : place + 1], (C, W))
    bias = jnp.broadcast_to(param_ref[:, place + 1 : place + 2], (C, W))
    plain, weighted = [], []
    for f in range(OWN):
        mean = jnp.broadcast_to(stats[f][0], (C, W))
        inverse = jnp.broadcast_to(stats[f][1], (C, W))
        sums = None
        for h in range(ROWS):
            normalized = (field_ref[f, h].astype(F32) - mean) * inverse
            pre = normalized * gain + bias
            sigmoid = 1.0 / (1.0 + jnp.exp(-pre))
            grad = upstream_ref[f, h] * (sigmoid * (1.0 + pre * (1.0 - sigmoid))) * gain
            grad_ref[f, h] = grad
            if active_ref is not None:
                active_ref[f, h] = (pre * sigmoid).astype(BF16)
            pair = (grad, grad * normalized)
            sums = pair if sums is None else (sums[0] + pair[0], sums[1] + pair[1])
        plain.append(jnp.sum(sums[0], axis=1, keepdims=True))
        weighted.append(jnp.sum(sums[1], axis=1, keepdims=True))
    return to_groups(plain + weighted)


def norm_two_kernel(
    own_ref, a_ref, b_ref, c_ref, field_ref, upstream_ref, param_ref, active_ref, grad_ref, stats_ref, out_ref
):
    parts = [ref[...] for ref in (own_ref, a_ref, b_ref, c_ref)]
    merged = stats_table(*merge(parts, 4 * LOCAL_COUNT))
    stats_ref[...] = merged
    wide = to_channels(merged)
    stats = [(wide[:, f : f + 1], wide[:, 4 + f : 5 + f]) for f in range(OWN)]
    out_ref[...] = norm_grad(stats, field_ref, upstream_ref, param_ref, grad_ref, 2, active_ref)


def field_grad(stats, sums, grad_ref, field_ref, finish):
    totals = to_channels(sums * (1.0 / FULL_COUNT))
    for f in range(OWN):
        mean = jnp.broadcast_to(stats[f][0], (C, W))
        inverse = jnp.broadcast_to(stats[f][1], (C, W))
        plain = jnp.broadcast_to(totals[:, f : f + 1], (C, W))
        weighted = jnp.broadcast_to(totals[:, OWN + f : OWN + f + 1], (C, W))
        for h in range(ROWS):
            normalized = (field_ref[f, h].astype(F32) - mean) * inverse
            finish(f, h, inverse * (grad_ref[f, h] - plain - normalized * weighted))


def grad_conv_kernel(stats_ref, own_ref, a_ref, b_ref, c_ref, grad_ref, field_ref, out_ref):
    def finish(f, h, value):
        out_ref[f, h] = value.astype(BF16)

    wide = to_channels(stats_ref[...])
    stats = [(wide[:, f : f + 1], wide[:, 4 + f : 5 + f]) for f in range(OWN)]
    field_grad(stats, own_ref[...] + a_ref[...] + b_ref[...] + c_ref[...], grad_ref, field_ref, finish)


def input_grad_kernel(stats_ref, own_ref, a_ref, b_ref, c_ref, grad_ref, field_ref, cot_ref, out_ref):
    def finish(f, h, value):
        out_ref[f, h] = (cot_ref[f, h].astype(F32) + value).astype(BF16)

    wide = to_channels(stats_ref[...])
    stats = [(wide[:, 2 + f : 3 + f], wide[:, 6 + f : 7 + f]) for f in range(OWN)]
    field_grad(stats, own_ref[...] + a_ref[...] + b_ref[...] + c_ref[...], grad_ref, field_ref, finish)


def weight_kernel(table_ref, cols_ref, grad_ref, kept_ref, send_ref, dense_ref, turned_ref):
    for h in range(ROWS):
        for f in range(OWN):
            block = grad_ref[f, h].T
            start = (h * OWN + f) * W
            turned_ref[2, start : start + W, :] = block
            wide = block.astype(F32)
            for k in range(2):
                at = (2 - k) * 4 + f
                turned_ref[k, start : start + W, :] = (wide * table_ref[at : at + 1, 0:1]).astype(BF16)
    for k in range(3):
        for spot in range(9):
            start = spot * C
            rows = [
                cols_ref[h * TAP_ROWS + start : h * TAP_ROWS + start + C, k * W : (k + 2) * W]
                for h in range(ROWS)
            ]
            dense_ref[k * DEPTH + start : k * DEPTH + start + C, :] = jnp.dot(
                jnp.concatenate(rows, axis=1), turned_ref[k], preferred_element_type=F32
            )
    half = SHARE // 2
    first = jnp.broadcast_to(table_ref[14:15, :], (HALF, W)) < 0.5
    for s in range(SPACE):
        low = dense_ref[s * SHARE : (s + 1) * SHARE, 0:W]
        high = jnp.concatenate(
            [
                dense_ref[s * SHARE : s * SHARE + half, W:C],
                dense_ref[s * SHARE + half : (s + 1) * SHARE, W:C],
            ],
            axis=1,
        )
        spare = jnp.zeros((PACKED - SHARE - half, W), F32)
        packed = jnp.concatenate([low, high, spare], axis=0).astype(BF16)
        kept_ref[s] = jnp.where(first, packed[:HALF], packed[HALF:])
        send_ref[s] = jnp.where(first, packed[HALF:], packed[:HALF])


def conv_two_kernel(
    table_ref, own_ref, prev_ref, inner_ref, outer_ref, weight_ref, input_ref, decoded_ref, cols_ref
):
    for f in range(4):
        ends = beside(table_ref, inner_ref, outer_ref, f)
        for h in range(ROWS + 2):
            if h == 0:
                field = ends[0]
            elif h == ROWS + 1:
                field = ends[1]
            else:
                field = (prev_ref if f < OWN else own_ref)[f % OWN, h - 1].astype(F32)
            store_shifted(cols_ref, h, f, field)

    def finish(h, total):
        for f in range(OWN):
            field = input_ref[f, h].astype(F32) + total[:, f * W : (f + 1) * W]
            decoded_ref[f, h] = field.astype(BF16)

    forward_conv(table_ref, weight_ref, cols_ref, finish)


def pair_kernel(kept_one_ref, came_one_ref, kept_two_ref, came_two_ref, out_ref, done_ref):
    for i, (kept, came) in enumerate(((kept_one_ref, came_one_ref), (kept_two_ref, came_two_ref))):
        out_ref[:, i * HALF : (i + 1) * HALF] = (kept[...].astype(F32) + came[...].astype(F32)).astype(BF16)
    done_ref[...] = jnp.zeros((8, W), F32)


def gather_kernel(parts_ref, out_ref):
    for i in range(2):
        rows = slice(i * HALF, (i + 1) * HALF)
        total = parts_ref[0, rows].astype(F32)
        for s in range(1, SPACE):
            total = total + parts_ref[s, rows].astype(F32)
        out_ref[i] = total.astype(BF16)


def chips_kernel(place_ref, own_ref, a_ref, b_ref, c_ref, out_ref, room_ref):
    for d, ref in enumerate((own_ref, a_ref, b_ref, c_ref)):
        room_ref[lax.rem(place_ref[0] + d, CHIPS)] = ref[...]
    total = room_ref[0].astype(F32)
    for x in range(1, CHIPS):
        total = total + room_ref[x].astype(F32)
    out_ref[...] = total


def unpack_kernel(table_ref, own_ref, came_ref, *out_refs, scale):
    second = jnp.broadcast_to(table_ref[14:15, :], (HALF, W)) > 0.5
    half = SHARE // 2
    for i, out_ref in enumerate(out_refs):
        own, came = own_ref[i] * scale, came_ref[i] * scale
        packed = jnp.concatenate([jnp.where(second, came, own), jnp.where(second, own, came)], axis=0)
        high = packed[SHARE : SHARE + half]
        out_ref[0:W, :] = packed[0:SHARE].T
        out_ref[W:C, 0:half] = high[:, : C - W].T
        out_ref[W:C, half:SHARE] = high[:, C - W :].T


def table_kernel(lengths_ref, out_ref):
    place, row = lax.axis_index("tm"), lax.axis_index("space")
    ends, end = [], 0
    for i in range(CLIPS):
        end = end + lengths_ref[i]
        ends.append(end)

    def clip_of(frame):
        return sum((frame >= end).astype(jnp.int32) for end in ends)

    values = []
    for lag in range(3):
        for f in range(4):
            frame = place * OWN + f
            kept = (frame >= lag) & (clip_of(frame - lag) == clip_of(frame))
            values.append(kept.astype(F32) if lag else jnp.float32(1.0))
    flags = (row > 0, row < SPACE - 1, place % 2 > 0, row % 2 > 0)
    for i, value in enumerate(values + [flag.astype(F32) for flag in flags]):
        out_ref[i : i + 1, :] = jnp.full((1, W), value, F32)


FORWARD = [(i, i + 1) for i in range(TM - 1)]
BACKWARD = [(i + 1, i) for i in range(TM - 1)]
INNER = [(i, i ^ 1) for i in range(SPACE)]
OUTER = [(i, ((i - 1) ^ 1) + 1 if 0 < i < SPACE - 1 else SPACE - 1 - i) for i in range(SPACE)]
SIBLING = [(i, i ^ 1) for i in range(TM)]


def edge_rows(table, *blocks, after=()):
    rows = shape((OWN * len(blocks), C, W), BF16)
    return call(edges_kernel, (rows, rows), (table, *blocks), after=after)


def row_halos(inner, outer):
    return lax.ppermute(inner, "space", INNER), lax.ppermute(outer, "space", OUTER)


SIDE = 4


def along(part, stride):
    near = [
        [(i, i - (i // stride % SIDE) * stride + ((i // stride + d) % SIDE) * stride) for i in range(SPACE)]
        for d in range(1, SIDE)
    ]
    return (part, *(lax.ppermute(part, "space", route) for route in near))


def shape(dims, dtype=F32):
    return jax.ShapeDtypeStruct(dims, dtype)


FIELD = (OWN, ROWS, C, W)
COLS = (6 * TAP_ROWS, 4 * W)


def shards(
    activations,
    weight_one,
    weight_two,
    gain_one,
    bias_one,
    gain_two,
    bias_two,
    cotangent,
    clip_lengths,
):
    table = pl.pallas_call(
        table_kernel,
        out_shape=shape((16, W)),
        in_specs=[pl.BlockSpec(memory_space=pltpu.SMEM)],
        out_specs=pl.BlockSpec(memory_space=pltpu.VMEM),
        compiler_params=pltpu.CompilerParams(vmem_limit_bytes=1024 * 1024),
    )(clip_lengths)
    params = jnp.stack([gain_one, bias_one, gain_two, bias_two], axis=1)
    turned_one, turned_two = weight_one.T, weight_two.T
    small = shape((8, W))
    turned = pltpu.VMEM((3, C, DEPTH), BF16)
    packed = shape((SPACE, HALF, W), BF16)
    dense = [pltpu.VMEM((ALL_TAPS, C), F32), pltpu.VMEM((3, OWN * ROWS * W, C), BF16)]

    fields, part = call(stats_kernel, (shape(FIELD, BF16), small), (activations,))
    part, upstream = call(
        join_kernel, (small, shape(FIELD, BF16)), (lax.ppermute(part, "tm", FORWARD), part, cotangent)
    )
    previous = lax.ppermute(fields, "tm", FORWARD)
    following = lax.ppermute(upstream, "tm", BACKWARD)
    merged = call(merge_kernel, small, along(part, 1))
    parts_one = along(merged, SIDE)
    inner, outer = row_halos(*edge_rows(table, previous, fields, upstream, following, after=(merged,)))
    columns_one, conv_one, stats_one, part = call(
        conv_one_kernel,
        (shape(COLS, BF16), shape(FIELD), small, small),
        (table, *parts_one, fields, previous, inner, outer, params, turned_one),
        limit=12,
    )
    merged = call(merge_kernel, small, along(part, 1))
    parts_two = along(merged, SIDE)
    grad_active_two = call(
        adjoint_two_kernel,
        shape(FIELD),
        (table, upstream, following, inner, outer, turned_two),
        scratch=[pltpu.VMEM(COLS, BF16), turned],
        after=(merged,),
        limit=16,
    )
    active_two, grad_norm, stats_two, part = call(
        norm_two_kernel,
        (shape(FIELD, BF16), shape(FIELD), small, small),
        (*parts_two, conv_one, grad_active_two, params),
    )
    merged = call(sum_kernel, small, along(part, 1))
    sums_two = along(merged, SIDE)
    active_two = call(copy_kernel, shape(FIELD, BF16), (active_two,), after=(merged,))
    previous_two = lax.ppermute(active_two, "tm", FORWARD)
    grad_conv_one = call(grad_conv_kernel, shape(FIELD, BF16), (stats_two, *sums_two, grad_norm, conv_one))
    following_one = lax.ppermute(grad_conv_one, "tm", BACKWARD)
    edges_two = edge_rows(table, previous_two, active_two, after=(grad_conv_one,))
    inner_two, outer_two = row_halos(*edges_two)
    kept_one, sent_one = call(
        weight_kernel,
        (packed, packed),
        (table, columns_one, grad_conv_one),
        scratch=dense,
        after=(edges_two[0],),
        limit=16,
    )
    came_one = lax.ppermute(sent_one, "tm", SIBLING)
    edges_one = edge_rows(table, grad_conv_one, following_one, after=(sent_one,))
    inner_one, outer_one = row_halos(*edges_one)
    decoded, columns_two = call(
        conv_two_kernel,
        (shape(FIELD, BF16), shape(COLS, BF16)),
        (table, active_two, previous_two, inner_two, outer_two, turned_two, fields),
        after=(edges_one[0],),
        limit=12,
    )
    kept_two, sent_two = call(
        weight_kernel,
        (packed, packed),
        (table, columns_two, upstream),
        scratch=dense,
        after=(inner_one, outer_one),
        limit=16,
    )
    came_two = lax.ppermute(sent_two, "tm", SIBLING)
    pairs, done_pairs = call(
        pair_kernel,
        (shape((SPACE, PACKED, W), BF16), small),
        (kept_one, came_one, kept_two, came_two),
    )
    swapped = lax.all_to_all(pairs, "space", 0, 0)
    grad_norm, part = call(
        adjoint_one_kernel,
        (shape(FIELD), small),
        (table, grad_conv_one, following_one, inner_one, outer_one, turned_one, stats_one, fields, params),
        scratch=[pltpu.VMEM(COLS, BF16), turned, pltpu.VMEM(FIELD, F32)],
        after=(done_pairs,),
        limit=16,
    )
    merged = call(sum_kernel, small, along(part, 1))
    sums_one = along(merged, SIDE)
    half = call(gather_kernel, shape((2, HALF, W), BF16), (swapped,), after=sums_one[1:])
    routes = [[(i, (i - 2 * d) % TM) for i in range(TM)] for d in range(1, CHIPS)]
    halves = (half, *(lax.ppermute(half, "tm", route) for route in routes))
    input_grad = call(
        input_grad_kernel, shape(FIELD, BF16), (stats_one, *sums_one, grad_norm, fields, upstream)
    )
    half = call(
        chips_kernel,
        shape((2, HALF, W)),
        ((lax.axis_index("tm") // 2).astype(jnp.int32).reshape(1), *halves),
        scratch=[pltpu.VMEM((CHIPS, 2, HALF, W), BF16)],
        smem=1,
    )
    total_cells = OWN * TM * ROWS * SPACE * W
    share_one, share_two = call(
        functools.partial(unpack_kernel, scale=float(total_cells) ** -0.5),
        (shape((C, SHARE)),) * 2,
        (table, half, lax.ppermute(half, "tm", SIBLING)),
    )
    return (decoded, input_grad, share_one.T, share_two.T)


def solution(mesh):
    placed = (
        P("tm", "space", None, None),
        P(),
        P(),
        P(),
        P(),
        P(),
        P(),
        P("tm", "space", None, None),
        P(),
    )
    return jax.shard_map(
        shards,
        mesh=mesh,
        in_specs=placed,
        out_specs=(
            P("tm", "space", None, None),
            P("tm", "space", None, None),
            P("space", None),
            P("space", None),
        ),
        check_vma=False,
    )
```

```python
import functools

import jax
import jax.numpy as jnp
from jax import lax
from jax.experimental import pallas as pl
from jax.experimental.pallas import tpu as pltpu
from jax.sharding import PartitionSpec as P

GROUPS = 32
NORM_EPSILON = 1e-05

C = 192
W = 128
PER_GROUP = C // GROUPS
ROWS = 4
OWN = 2
TAP_ROWS = 3 * C
DEPTH = 3 * TAP_ROWS
ALL_TAPS = 3 * DEPTH
SPACE = 16
TM = 8
CLIPS = 4
SHARE = ALL_TAPS // SPACE
PACKED = 512
HALF = PACKED // 2
CHIPS = TM // 2
LOCAL_COUNT = ROWS * PER_GROUP * W
FULL_COUNT = LOCAL_COUNT * SPACE

F32 = jnp.float32
BF16 = jnp.bfloat16
EXACT = lax.Precision.HIGHEST


def call(kernel, out_shape, operands, scratch=(), after=(), limit=8, smem=0, us=0):
    count, extra = len(operands), len(after)

    def body(*refs):
        kernel(*refs[:count], *refs[count + extra :])

    return pl.pallas_call(
        body,
        out_shape=out_shape,
        in_specs=[pl.BlockSpec(memory_space=pltpu.SMEM)] * smem
        + [pl.BlockSpec(memory_space=pltpu.VMEM)] * (count - smem)
        + [pl.BlockSpec(memory_space=pl.ANY)] * extra,
        out_specs=jax.tree.map(lambda _: pl.BlockSpec(memory_space=pltpu.VMEM), out_shape),
        scratch_shapes=list(scratch),
        compiler_params=pltpu.CompilerParams(vmem_limit_bytes=limit * 1024 * 1024),
        cost_estimate=pl.CostEstimate(flops=0, bytes_accessed=us * 3600000, transcendentals=0),
    )(*operands, *after)


def lane_ids(rows=C):
    return lax.broadcasted_iota(jnp.int32, (rows, W), 1)


def membership():
    channel = lax.broadcasted_iota(jnp.int32, (C, W), 0)
    group = lane_ids()
    inside = (channel >= group * PER_GROUP) & (channel < (group + 1) * PER_GROUP)
    return inside.astype(F32)


def to_groups(columns):
    lanes = lane_ids()
    packed = jnp.zeros((C, W), F32)
    for i, column in enumerate(columns):
        packed = jnp.where(lanes == i, column, packed)
    summed = lax.dot_general(
        packed, membership(), (((0,), (0,)), ((), ())), precision=EXACT, preferred_element_type=F32
    )
    return summed[:8]


def to_channels(table):
    return lax.dot_general(
        membership(), table, (((1,), (1,)), ((), ())), precision=EXACT, preferred_element_type=F32
    )


def merge(parts, count):
    mean = sum(part[0:4] for part in parts) * (1.0 / len(parts))
    spread = sum((part[0:4] - mean) ** 2 for part in parts) * float(count)
    return mean, sum(part[4:8] for part in parts) + spread


def stats_table(mean, squares):
    return jnp.concatenate([mean, lax.rsqrt(squares * (1.0 / FULL_COUNT) + NORM_EPSILON)], axis=0)


def local_stats(blocks):
    sums = []
    for rows in blocks:
        total = rows[0]()
        for row in rows[1:]:
            total = total + row()
        sums.append(jnp.sum(total, axis=1, keepdims=True))
    means = to_groups(sums) * (1.0 / LOCAL_COUNT)
    spread = to_channels(means)
    squares = []
    for f, rows in enumerate(blocks):
        total = None
        for row in rows:
            centered = row() - spread[:, f : f + 1]
            total = centered * centered if total is None else total + centered * centered
        squares.append(jnp.sum(total, axis=1, keepdims=True))
    deviations = to_groups(squares)
    return jnp.concatenate([means[:4], deviations[:4]], axis=0)


def store_shifted(cols_ref, h, f, field):
    lanes = lane_ids()
    before = jnp.where(lanes == 0, 0.0, pltpu.roll(field, 1, 1))
    after = jnp.where(lanes == W - 1, 0.0, pltpu.roll(field, W - 1, 1))
    for s, part in enumerate((before, field, after)):
        start = h * TAP_ROWS + s * C
        cols_ref[start : start + C, f * W : (f + 1) * W] = part.astype(BF16)


def conv_rows(kernels, cols_ref, factors, finish):
    for h in range(ROWS):
        total = None
        for k in range(3):
            part = jnp.dot(
                kernels[k],
                cols_ref[h * TAP_ROWS : h * TAP_ROWS + DEPTH, k * W : (k + 2) * W],
                preferred_element_type=F32,
            )
            if factors[k] is not None:
                part = part * factors[k]
            total = part if total is None else total + part
        finish(h, total)


def factor(table_ref, lag, frame):
    at = lag * 4 + frame
    return jnp.concatenate([table_ref[at : at + 1, :], table_ref[at + 1 : at + 2, :]], axis=1)


def edges_kernel(table_ref, *refs):
    odd = jnp.broadcast_to(table_ref[15:16, :], (C, W)) > 0.5
    inner_ref, outer_ref = refs[-2:]
    for i, ref in enumerate(refs[:-2]):
        for f in range(OWN):
            low, high = ref[f, ROWS - 1].astype(F32), ref[f, 0].astype(F32)
            inner_ref[i * OWN + f] = jnp.where(odd, high, low).astype(BF16)
            outer_ref[i * OWN + f] = jnp.where(odd, low, high).astype(BF16)


def beside(table_ref, inner_ref, outer_ref, i):
    odd = jnp.broadcast_to(table_ref[15:16, :], (C, W)) > 0.5
    inner, outer = inner_ref[i].astype(F32), outer_ref[i].astype(F32)
    above = jnp.where(odd, inner, outer) * table_ref[12:13, :]
    below = jnp.where(odd, outer, inner) * table_ref[13:14, :]
    return above, below


def stats_kernel(own_ref, copy_ref, out_ref):
    def row(f, h):
        return lambda: own_ref[f, h].astype(F32)

    out_ref[...] = local_stats([[row(f, h) for h in range(ROWS)] for f in range(OWN)])
    copy_ref[...] = own_ref[...]


def copy_kernel(src_ref, out_ref):
    out_ref[...] = src_ref[...]


def join_kernel(prev_ref, own_ref, cot_ref, out_ref, copy_ref):
    for i, ref in enumerate((prev_ref, own_ref)):
        out_ref[i * OWN : (i + 1) * OWN] = ref[0:OWN]
        out_ref[4 + i * OWN : 4 + (i + 1) * OWN] = ref[4 : 4 + OWN]
    copy_ref[...] = cot_ref[...]


def silu_of(pre):
    return pre / (1.0 + jnp.exp(-pre))


def active_columns(cols_ref, table_ref, stats, gain, bias, own, prev, inner, outer):
    shift = jnp.broadcast_to(bias, (C, W))
    for f in range(4):
        mean = jnp.broadcast_to(stats[f][0], (C, W))
        scale = jnp.broadcast_to(stats[f][1] * gain, (C, W))
        ends = beside(table_ref, inner, outer, f)
        for h in range(ROWS + 2):
            if h == 0:
                field = ends[0]
            elif h == ROWS + 1:
                field = ends[1]
            else:
                field = (prev if f < OWN else own)[f % OWN, h - 1].astype(F32)
            active = silu_of((field - mean) * scale + shift)
            if h == 0:
                active = active * table_ref[12:13, :]
            if h == ROWS + 1:
                active = active * table_ref[13:14, :]
            store_shifted(cols_ref, h, f, active)


def forward_conv(table_ref, weight_ref, cols_ref, finish):
    kernels = [weight_ref[:, k * DEPTH : (k + 1) * DEPTH] for k in range(3)]
    factors = [factor(table_ref, 2 - k, 0) for k in range(2)] + [None]
    conv_rows(kernels, cols_ref, factors, finish)


def conv_one_kernel(
    table_ref, part_ref, a_ref, b_ref, c_ref, own_ref, prev_ref, inner_ref, outer_ref, param_ref, weight_ref,
    cols_ref, conv_ref, stats_ref, out_ref,
):
    parts = [ref[...] for ref in (part_ref, a_ref, b_ref, c_ref)]
    merged = stats_table(*merge(parts, 4 * LOCAL_COUNT))
    stats_ref[...] = merged
    wide = to_channels(merged)
    stats = [(wide[:, f : f + 1], wide[:, 4 + f : 5 + f]) for f in range(4)]
    active_columns(
        cols_ref, table_ref, stats, param_ref[:, 0:1], param_ref[:, 1:2], own_ref, prev_ref, inner_ref, outer_ref
    )

    def finish(h, total):
        for f in range(OWN):
            conv_ref[f, h] = total[:, f * W : (f + 1) * W]

    forward_conv(table_ref, weight_ref, cols_ref, finish)

    def row(f, h):
        return lambda: conv_ref[f, h]

    out_ref[...] = local_stats([[row(f, h) for h in range(ROWS)] for f in range(OWN)])


def merge_kernel(own_ref, a_ref, b_ref, c_ref, out_ref):
    mean, squares = merge([ref[...] for ref in (own_ref, a_ref, b_ref, c_ref)], LOCAL_COUNT)
    out_ref[...] = jnp.concatenate([mean, squares], axis=0)


def sum_kernel(own_ref, a_ref, b_ref, c_ref, out_ref):
    out_ref[...] = own_ref[...] + a_ref[...] + b_ref[...] + c_ref[...]


def turn(src_ref, dst_ref):
    row = lax.broadcasted_iota(jnp.int32, (C, C), 0)
    eye = (row == lax.broadcasted_iota(jnp.int32, (C, C), 1)).astype(BF16)
    for tap in range(27):
        k, spot = divmod(26 - tap, 9)
        block = lax.dot_general(
            eye, src_ref[:, tap * C : (tap + 1) * C], (((1,), (1,)), ((), ())), preferred_element_type=F32
        )
        dst_ref[k, :, spot * C : (spot + 1) * C] = block.astype(BF16)


def adjoint(table_ref, own_ref, next_ref, inner_ref, outer_ref, weight_ref, out_ref, cols_ref, turned_ref, first):
    for f in range(4):
        ends = beside(table_ref, inner_ref, outer_ref, first + f)
        for h in range(ROWS + 2):
            if h == 0:
                field = ends[0]
            elif h == ROWS + 1:
                field = ends[1]
            else:
                field = (own_ref if f < OWN else next_ref)[f % OWN, h - 1].astype(F32)
            store_shifted(cols_ref, h, f, field)
    turn(weight_ref, turned_ref)
    factors = [None] + [factor(table_ref, j, j) for j in (1, 2)]

    def finish(h, total):
        out_ref[0, h] = total[:, :W]
        out_ref[1, h] = total[:, W:]

    conv_rows([turned_ref[j] for j in range(3)], cols_ref, factors, finish)


def adjoint_two_kernel(
    table_ref, own_ref, next_ref, inner_ref, outer_ref, weight_ref, out_ref, cols_ref, turned_ref
):
    adjoint(table_ref, own_ref, next_ref, inner_ref, outer_ref, weight_ref, out_ref, cols_ref, turned_ref, 4)


def adjoint_one_kernel(
    table_ref, own_ref, next_ref, inner_ref, outer_ref, weight_ref, stats_ref, field_ref, param_ref,
    grad_ref, out_ref, cols_ref, turned_ref, upstream_ref,
):
    adjoint(
        table_ref, own_ref, next_ref, inner_ref, outer_ref, weight_ref, upstream_ref, cols_ref, turned_ref, 0
    )
    wide = to_channels(stats_ref[...])
    stats = [(wide[:, 2 + f : 3 + f], wide[:, 6 + f : 7 + f]) for f in range(OWN)]
    out_ref[...] = norm_grad(stats, field_ref, upstream_ref, param_ref, grad_ref, 0)


def norm_grad(stats, field_ref, upstream_ref, param_ref, grad_ref, place, active_ref=None):
    gain = jnp.broadcast_to(param_ref[:, place : place + 1], (C, W))
    bias = jnp.broadcast_to(param_ref[:, place + 1 : place + 2], (C, W))
    plain, weighted = [], []
    for f in range(OWN):
        mean = jnp.broadcast_to(stats[f][0], (C, W))
        inverse = jnp.broadcast_to(stats[f][1], (C, W))
        sums = None
        for h in range(ROWS):
            normalized = (field_ref[f, h].astype(F32) - mean) * inverse
            pre = normalized * gain + bias
            sigmoid = 1.0 / (1.0 + jnp.exp(-pre))
            grad = upstream_ref[f, h] * (sigmoid * (1.0 + pre * (1.0 - sigmoid))) * gain
            grad_ref[f, h] = grad
            if active_ref is not None:
                active_ref[f, h] = (pre * sigmoid).astype(BF16)
            pair = (grad, grad * normalized)
            sums = pair if sums is None else (sums[0] + pair[0], sums[1] + pair[1])
        plain.append(jnp.sum(sums[0], axis=1, keepdims=True))
        weighted.append(jnp.sum(sums[1], axis=1, keepdims=True))
    return to_groups(plain + weighted)


def norm_two_kernel(
    own_ref, a_ref, b_ref, c_ref, field_ref, upstream_ref, param_ref, active_ref, grad_ref, stats_ref, out_ref
):
    parts = [ref[...] for ref in (own_ref, a_ref, b_ref, c_ref)]
    merged = stats_table(*merge(parts, 4 * LOCAL_COUNT))
    stats_ref[...] = merged
    wide = to_channels(merged)
    stats = [(wide[:, f : f + 1], wide[:, 4 + f : 5 + f]) for f in range(OWN)]
    out_ref[...] = norm_grad(stats, field_ref, upstream_ref, param_ref, grad_ref, 2, active_ref)


def field_grad(stats, sums, grad_ref, field_ref, finish):
    totals = to_channels(sums * (1.0 / FULL_COUNT))
    for f in range(OWN):
        mean = jnp.broadcast_to(stats[f][0], (C, W))
        inverse = jnp.broadcast_to(stats[f][1], (C, W))
        plain = jnp.broadcast_to(totals[:, f : f + 1], (C, W))
        weighted = jnp.broadcast_to(totals[:, OWN + f : OWN + f + 1], (C, W))
        for h in range(ROWS):
            normalized = (field_ref[f, h].astype(F32) - mean) * inverse
            finish(f, h, inverse * (grad_ref[f, h] - plain - normalized * weighted))


def grad_conv_kernel(stats_ref, own_ref, a_ref, b_ref, c_ref, grad_ref, field_ref, out_ref):
    def finish(f, h, value):
        out_ref[f, h] = value.astype(BF16)

    wide = to_channels(stats_ref[...])
    stats = [(wide[:, f : f + 1], wide[:, 4 + f : 5 + f]) for f in range(OWN)]
    field_grad(stats, own_ref[...] + a_ref[...] + b_ref[...] + c_ref[...], grad_ref, field_ref, finish)


def input_grad_kernel(stats_ref, own_ref, a_ref, b_ref, c_ref, grad_ref, field_ref, cot_ref, out_ref, done_ref):
    def finish(f, h, value):
        out_ref[f, h] = (cot_ref[f, h].astype(F32) + value).astype(BF16)

    wide = to_channels(stats_ref[...])
    stats = [(wide[:, 2 + f : 3 + f], wide[:, 6 + f : 7 + f]) for f in range(OWN)]
    field_grad(stats, own_ref[...] + a_ref[...] + b_ref[...] + c_ref[...], grad_ref, field_ref, finish)
    done_ref[...] = jnp.zeros((8, W), F32)


def weight_kernel(table_ref, cols_ref, grad_ref, kept_ref, send_ref, dense_ref, turned_ref):
    for h in range(ROWS):
        for f in range(OWN):
            block = grad_ref[f, h].T
            start = (h * OWN + f) * W
            turned_ref[2, start : start + W, :] = block
            wide = block.astype(F32)
            for k in range(2):
                at = (2 - k) * 4 + f
                turned_ref[k, start : start + W, :] = (wide * table_ref[at : at + 1, 0:1]).astype(BF16)
    for k in range(3):
        for spot in range(9):
            start = spot * C
            rows = [
                cols_ref[h * TAP_ROWS + start : h * TAP_ROWS + start + C, k * W : (k + 2) * W]
                for h in range(ROWS)
            ]
            dense_ref[k * DEPTH + start : k * DEPTH + start + C, :] = jnp.dot(
                jnp.concatenate(rows, axis=1), turned_ref[k], preferred_element_type=F32
            )
    half = SHARE // 2
    first = jnp.broadcast_to(table_ref[14:15, :], (HALF, W)) < 0.5
    for s in range(SPACE):
        low = dense_ref[s * SHARE : (s + 1) * SHARE, 0:W]
        high = jnp.concatenate(
            [
                dense_ref[s * SHARE : s * SHARE + half, W:C],
                dense_ref[s * SHARE + half : (s + 1) * SHARE, W:C],
            ],
            axis=1,
        )
        spare = jnp.zeros((PACKED - SHARE - half, W), F32)
        packed = jnp.concatenate([low, high, spare], axis=0).astype(BF16)
        kept_ref[s] = jnp.where(first, packed[:HALF], packed[HALF:])
        send_ref[s] = jnp.where(first, packed[HALF:], packed[:HALF])


def conv_two_kernel(
    table_ref, own_ref, prev_ref, inner_ref, outer_ref, weight_ref, input_ref, decoded_ref, cols_ref
):
    for f in range(4):
        ends = beside(table_ref, inner_ref, outer_ref, f)
        for h in range(ROWS + 2):
            if h == 0:
                field = ends[0]
            elif h == ROWS + 1:
                field = ends[1]
            else:
                field = (prev_ref if f < OWN else own_ref)[f % OWN, h - 1].astype(F32)
            store_shifted(cols_ref, h, f, field)

    def finish(h, total):
        for f in range(OWN):
            field = input_ref[f, h].astype(F32) + total[:, f * W : (f + 1) * W]
            decoded_ref[f, h] = field.astype(BF16)

    forward_conv(table_ref, weight_ref, cols_ref, finish)


def pair_kernel(kept_one_ref, came_one_ref, kept_two_ref, came_two_ref, out_ref, done_ref):
    for i, (kept, came) in enumerate(((kept_one_ref, came_one_ref), (kept_two_ref, came_two_ref))):
        out_ref[:, i * HALF : (i + 1) * HALF] = (kept[...].astype(F32) + came[...].astype(F32)).astype(BF16)
    done_ref[...] = jnp.zeros((8, W), F32)


def gather_kernel(parts_ref, out_ref):
    for i in range(2):
        rows = slice(i * HALF, (i + 1) * HALF)
        total = parts_ref[0, rows].astype(F32)
        for s in range(1, SPACE):
            total = total + parts_ref[s, rows].astype(F32)
        out_ref[i] = total.astype(BF16)


def chips_kernel(place_ref, own_ref, a_ref, b_ref, c_ref, out_ref, room_ref):
    for d, ref in enumerate((own_ref, a_ref, b_ref, c_ref)):
        room_ref[lax.rem(place_ref[0] + d, CHIPS)] = ref[...]
    total = room_ref[0].astype(F32)
    for x in range(1, CHIPS):
        total = total + room_ref[x].astype(F32)
    out_ref[...] = total


def unpack_kernel(table_ref, own_ref, came_ref, *out_refs, scale):
    second = jnp.broadcast_to(table_ref[14:15, :], (HALF, W)) > 0.5
    half = SHARE // 2
    for i, out_ref in enumerate(out_refs):
        own, came = own_ref[i] * scale, came_ref[i] * scale
        packed = jnp.concatenate([jnp.where(second, came, own), jnp.where(second, own, came)], axis=0)
        high = packed[SHARE : SHARE + half]
        out_ref[0:W, :] = packed[0:SHARE].T
        out_ref[W:C, 0:half] = high[:, : C - W].T
        out_ref[W:C, half:SHARE] = high[:, C - W :].T


def table_kernel(lengths_ref, out_ref):
    place, row = lax.axis_index("tm"), lax.axis_index("space")
    ends, end = [], 0
    for i in range(CLIPS):
        end = end + lengths_ref[i]
        ends.append(end)

    def clip_of(frame):
        return sum((frame >= end).astype(jnp.int32) for end in ends)

    values = []
    for lag in range(3):
        for f in range(4):
            frame = place * OWN + f
            kept = (frame >= lag) & (clip_of(frame - lag) == clip_of(frame))
            values.append(kept.astype(F32) if lag else jnp.float32(1.0))
    flags = (row > 0, row < SPACE - 1, place % 2 > 0, row % 2 > 0)
    for i, value in enumerate(values + [flag.astype(F32) for flag in flags]):
        out_ref[i : i + 1, :] = jnp.full((1, W), value, F32)


FORWARD = [(i, i + 1) for i in range(TM - 1)]
BACKWARD = [(i + 1, i) for i in range(TM - 1)]
INNER = [(i, i ^ 1) for i in range(SPACE)]
OUTER = [(i, ((i - 1) ^ 1) + 1 if 0 < i < SPACE - 1 else SPACE - 1 - i) for i in range(SPACE)]
SIBLING = [(i, i ^ 1) for i in range(TM)]


def edge_rows(table, *blocks, after=()):
    rows = shape((OWN * len(blocks), C, W), BF16)
    return call(edges_kernel, (rows, rows), (table, *blocks), after=after)


def row_halos(inner, outer):
    return lax.ppermute(inner, "space", INNER), lax.ppermute(outer, "space", OUTER)


SIDE = 4


def along(part, stride):
    near = [
        [(i, i - (i // stride % SIDE) * stride + ((i // stride + d) % SIDE) * stride) for i in range(SPACE)]
        for d in range(1, SIDE)
    ]
    return (part, *(lax.ppermute(part, "space", route) for route in near))


def shape(dims, dtype=F32):
    return jax.ShapeDtypeStruct(dims, dtype)


FIELD = (OWN, ROWS, C, W)
COLS = (6 * TAP_ROWS, 4 * W)


def shards(
    activations,
    weight_one,
    weight_two,
    gain_one,
    bias_one,
    gain_two,
    bias_two,
    cotangent,
    clip_lengths,
):
    table = pl.pallas_call(
        table_kernel,
        out_shape=shape((16, W)),
        in_specs=[pl.BlockSpec(memory_space=pltpu.SMEM)],
        out_specs=pl.BlockSpec(memory_space=pltpu.VMEM),
        compiler_params=pltpu.CompilerParams(vmem_limit_bytes=1024 * 1024),
    )(clip_lengths)
    params = jnp.stack([gain_one, bias_one, gain_two, bias_two], axis=1)
    turned_one, turned_two = weight_one.T, weight_two.T
    small = shape((8, W))
    turned = pltpu.VMEM((3, C, DEPTH), BF16)
    packed = shape((SPACE, HALF, W), BF16)
    dense = [pltpu.VMEM((ALL_TAPS, C), F32), pltpu.VMEM((3, OWN * ROWS * W, C), BF16)]

    fields, part = call(stats_kernel, (shape(FIELD, BF16), small), (activations,))
    part, upstream = call(
        join_kernel, (small, shape(FIELD, BF16)), (lax.ppermute(part, "tm", FORWARD), part, cotangent)
    )
    previous = lax.ppermute(fields, "tm", FORWARD)
    following = lax.ppermute(upstream, "tm", BACKWARD)
    merged = call(merge_kernel, small, along(part, 1))
    parts_one = along(merged, SIDE)
    inner, outer = row_halos(*edge_rows(table, previous, fields, upstream, following, after=(merged,)))
    columns_one, conv_one, stats_one, part = call(
        conv_one_kernel,
        (shape(COLS, BF16), shape(FIELD), small, small),
        (table, *parts_one, fields, previous, inner, outer, params, turned_one),
        limit=12,
    )
    merged = call(merge_kernel, small, along(part, 1))
    parts_two = along(merged, SIDE)
    grad_active_two = call(
        adjoint_two_kernel,
        shape(FIELD),
        (table, upstream, following, inner, outer, turned_two),
        scratch=[pltpu.VMEM(COLS, BF16), turned],
        after=(merged,),
        limit=16,
    )
    active_two, grad_norm, stats_two, part = call(
        norm_two_kernel,
        (shape(FIELD, BF16), shape(FIELD), small, small),
        (*parts_two, conv_one, grad_active_two, params),
    )
    merged = call(sum_kernel, small, along(part, 1))
    sums_two = along(merged, SIDE)
    active_two = call(copy_kernel, shape(FIELD, BF16), (active_two,), after=(merged,))
    previous_two = lax.ppermute(active_two, "tm", FORWARD)
    grad_conv_one = call(grad_conv_kernel, shape(FIELD, BF16), (stats_two, *sums_two, grad_norm, conv_one))
    following_one = lax.ppermute(grad_conv_one, "tm", BACKWARD)
    edges_two = edge_rows(table, previous_two, active_two, after=(grad_conv_one,))
    inner_two, outer_two = row_halos(*edges_two)
    kept_one, sent_one = call(
        weight_kernel,
        (packed, packed),
        (table, columns_one, grad_conv_one),
        scratch=dense,
        after=(edges_two[0],),
        limit=16,
    )
    came_one = lax.ppermute(sent_one, "tm", SIBLING)
    edges_one = edge_rows(table, grad_conv_one, following_one, after=(sent_one,))
    inner_one, outer_one = row_halos(*edges_one)
    decoded, columns_two = call(
        conv_two_kernel,
        (shape(FIELD, BF16), shape(COLS, BF16)),
        (table, active_two, previous_two, inner_two, outer_two, turned_two, fields),
        after=(edges_one[0],),
        limit=12,
    )
    kept_two, sent_two = call(
        weight_kernel,
        (packed, packed),
        (table, columns_two, upstream),
        scratch=dense,
        after=(inner_one, outer_one),
        limit=16,
    )
    came_two = lax.ppermute(sent_two, "tm", SIBLING)
    pairs, done_pairs = call(
        pair_kernel,
        (shape((SPACE, PACKED, W), BF16), small),
        (kept_one, came_one, kept_two, came_two),
    )
    swapped = lax.all_to_all(pairs, "space", 0, 0)
    grad_norm, part = call(
        adjoint_one_kernel,
        (shape(FIELD), small),
        (table, grad_conv_one, following_one, inner_one, outer_one, turned_one, stats_one, fields, params),
        scratch=[pltpu.VMEM(COLS, BF16), turned, pltpu.VMEM(FIELD, F32)],
        after=(done_pairs,),
        limit=16,
    )
    merged = call(sum_kernel, small, along(part, 1))
    sums_one = along(merged, SIDE)
    half = call(gather_kernel, shape((2, HALF, W), BF16), (swapped,), after=sums_one[1:])
    routes = [[(i, (i - 2 * d) % TM) for i in range(TM)] for d in range(1, CHIPS)]
    halves = (half, *(lax.ppermute(half, "tm", route) for route in routes))
    input_grad, done_grad = call(
        input_grad_kernel,
        (shape(FIELD, BF16), small),
        (stats_one, *sums_one, grad_norm, fields, upstream),
        us=3,
    )
    half = call(
        chips_kernel,
        shape((2, HALF, W)),
        ((lax.axis_index("tm") // 2).astype(jnp.int32).reshape(1), *halves),
        scratch=[pltpu.VMEM((CHIPS, 2, HALF, W), BF16)],
        smem=1,
        after=(done_grad,),
    )
    total_cells = OWN * TM * ROWS * SPACE * W
    share_one, share_two = call(
        functools.partial(unpack_kernel, scale=float(total_cells) ** -0.5),
        (shape((C, SHARE)),) * 2,
        (table, half, lax.ppermute(half, "tm", SIBLING)),
    )
    return (decoded, input_grad, share_one.T, share_two.T)


def solution(mesh):
    placed = (
        P("tm", "space", None, None),
        P(),
        P(),
        P(),
        P(),
        P(),
        P(),
        P("tm", "space", None, None),
        P(),
    )
    return jax.shard_map(
        shards,
        mesh=mesh,
        in_specs=placed,
        out_specs=(
            P("tm", "space", None, None),
            P("tm", "space", None, None),
            P("space", None),
            P("space", None),
        ),
        check_vma=False,
    )
```

```python
import functools

import jax
import jax.numpy as jnp
from jax import lax
from jax.experimental import pallas as pl
from jax.experimental.pallas import tpu as pltpu
from jax.sharding import PartitionSpec as P

GROUPS = 32
NORM_EPSILON = 1e-05

C = 192
W = 128
PER_GROUP = C // GROUPS
ROWS = 4
OWN = 2
TAP_ROWS = 3 * C
DEPTH = 3 * TAP_ROWS
ALL_TAPS = 3 * DEPTH
SPACE = 16
TM = 8
CLIPS = 4
SHARE = ALL_TAPS // SPACE
PACKED = 512
HALF = PACKED // 2
CHIPS = TM // 2
LOCAL_COUNT = ROWS * PER_GROUP * W
FULL_COUNT = LOCAL_COUNT * SPACE

F32 = jnp.float32
BF16 = jnp.bfloat16
EXACT = lax.Precision.HIGHEST


def call(kernel, out_shape, operands, scratch=(), after=(), limit=8, smem=0, us=0):
    count, extra = len(operands), len(after)

    def body(*refs):
        kernel(*refs[:count], *refs[count + extra :])

    return pl.pallas_call(
        body,
        out_shape=out_shape,
        in_specs=[pl.BlockSpec(memory_space=pltpu.SMEM)] * smem
        + [pl.BlockSpec(memory_space=pltpu.VMEM)] * (count - smem)
        + [pl.BlockSpec(memory_space=pl.ANY)] * extra,
        out_specs=jax.tree.map(lambda _: pl.BlockSpec(memory_space=pltpu.VMEM), out_shape),
        scratch_shapes=list(scratch),
        compiler_params=pltpu.CompilerParams(vmem_limit_bytes=limit * 1024 * 1024),
        cost_estimate=pl.CostEstimate(flops=0, bytes_accessed=us * 3600000, transcendentals=0),
    )(*operands, *after)


def lane_ids(rows=C):
    return lax.broadcasted_iota(jnp.int32, (rows, W), 1)


def membership():
    channel = lax.broadcasted_iota(jnp.int32, (C, W), 0)
    group = lane_ids()
    inside = (channel >= group * PER_GROUP) & (channel < (group + 1) * PER_GROUP)
    return inside.astype(F32)


def to_groups(columns):
    lanes = lane_ids()
    packed = jnp.zeros((C, W), F32)
    for i, column in enumerate(columns):
        packed = jnp.where(lanes == i, column, packed)
    summed = lax.dot_general(
        packed, membership(), (((0,), (0,)), ((), ())), precision=EXACT, preferred_element_type=F32
    )
    return summed[:8]


def to_channels(table):
    return lax.dot_general(
        membership(), table, (((1,), (1,)), ((), ())), precision=EXACT, preferred_element_type=F32
    )


def merge(parts, count):
    mean = sum(part[0:4] for part in parts) * (1.0 / len(parts))
    spread = sum((part[0:4] - mean) ** 2 for part in parts) * float(count)
    return mean, sum(part[4:8] for part in parts) + spread


def stats_table(mean, squares):
    return jnp.concatenate([mean, lax.rsqrt(squares * (1.0 / FULL_COUNT) + NORM_EPSILON)], axis=0)


def local_stats(blocks):
    sums = []
    for rows in blocks:
        total = rows[0]()
        for row in rows[1:]:
            total = total + row()
        sums.append(jnp.sum(total, axis=1, keepdims=True))
    means = to_groups(sums) * (1.0 / LOCAL_COUNT)
    spread = to_channels(means)
    squares = []
    for f, rows in enumerate(blocks):
        total = None
        for row in rows:
            centered = row() - spread[:, f : f + 1]
            total = centered * centered if total is None else total + centered * centered
        squares.append(jnp.sum(total, axis=1, keepdims=True))
    deviations = to_groups(squares)
    return jnp.concatenate([means[:4], deviations[:4]], axis=0)


def store_shifted(cols_ref, h, f, field):
    lanes = lane_ids()
    before = jnp.where(lanes == 0, 0.0, pltpu.roll(field, 1, 1))
    after = jnp.where(lanes == W - 1, 0.0, pltpu.roll(field, W - 1, 1))
    for s, part in enumerate((before, field, after)):
        start = h * TAP_ROWS + s * C
        cols_ref[start : start + C, f * W : (f + 1) * W] = part.astype(BF16)


def conv_rows(kernels, cols_ref, factors, finish):
    for h in range(ROWS):
        total = None
        for k in range(3):
            part = jnp.dot(
                kernels[k],
                cols_ref[h * TAP_ROWS : h * TAP_ROWS + DEPTH, k * W : (k + 2) * W],
                preferred_element_type=F32,
            )
            if factors[k] is not None:
                part = part * factors[k]
            total = part if total is None else total + part
        finish(h, total)


def factor(table_ref, lag, frame):
    at = lag * 4 + frame
    return jnp.concatenate([table_ref[at : at + 1, :], table_ref[at + 1 : at + 2, :]], axis=1)


def edges_kernel(table_ref, *refs):
    odd = jnp.broadcast_to(table_ref[15:16, :], (C, W)) > 0.5
    inner_ref, outer_ref = refs[-2:]
    for i, ref in enumerate(refs[:-2]):
        for f in range(OWN):
            low, high = ref[f, ROWS - 1].astype(F32), ref[f, 0].astype(F32)
            inner_ref[i * OWN + f] = jnp.where(odd, high, low).astype(BF16)
            outer_ref[i * OWN + f] = jnp.where(odd, low, high).astype(BF16)


def beside(table_ref, inner_ref, outer_ref, i):
    odd = jnp.broadcast_to(table_ref[15:16, :], (C, W)) > 0.5
    inner, outer = inner_ref[i].astype(F32), outer_ref[i].astype(F32)
    above = jnp.where(odd, inner, outer) * table_ref[12:13, :]
    below = jnp.where(odd, outer, inner) * table_ref[13:14, :]
    return above, below


def stats_kernel(own_ref, copy_ref, out_ref):
    def row(f, h):
        return lambda: own_ref[f, h].astype(F32)

    out_ref[...] = local_stats([[row(f, h) for h in range(ROWS)] for f in range(OWN)])
    copy_ref[...] = own_ref[...]


def copy_kernel(src_ref, out_ref):
    out_ref[...] = src_ref[...]


def join_kernel(prev_ref, own_ref, cot_ref, out_ref, copy_ref):
    for i, ref in enumerate((prev_ref, own_ref)):
        out_ref[i * OWN : (i + 1) * OWN] = ref[0:OWN]
        out_ref[4 + i * OWN : 4 + (i + 1) * OWN] = ref[4 : 4 + OWN]
    copy_ref[...] = cot_ref[...]


def silu_of(pre):
    return pre / (1.0 + jnp.exp(-pre))


def active_columns(cols_ref, table_ref, stats, gain, bias, own, prev, inner, outer):
    shift = jnp.broadcast_to(bias, (C, W))
    for f in range(4):
        mean = jnp.broadcast_to(stats[f][0], (C, W))
        scale = jnp.broadcast_to(stats[f][1] * gain, (C, W))
        ends = beside(table_ref, inner, outer, f)
        for h in range(ROWS + 2):
            if h == 0:
                field = ends[0]
            elif h == ROWS + 1:
                field = ends[1]
            else:
                field = (prev if f < OWN else own)[f % OWN, h - 1].astype(F32)
            active = silu_of((field - mean) * scale + shift)
            if h == 0:
                active = active * table_ref[12:13, :]
            if h == ROWS + 1:
                active = active * table_ref[13:14, :]
            store_shifted(cols_ref, h, f, active)


def forward_conv(table_ref, weight_ref, cols_ref, finish):
    kernels = [weight_ref[:, k * DEPTH : (k + 1) * DEPTH] for k in range(3)]
    factors = [factor(table_ref, 2 - k, 0) for k in range(2)] + [None]
    conv_rows(kernels, cols_ref, factors, finish)


def conv_one_kernel(
    table_ref, part_ref, a_ref, b_ref, c_ref, own_ref, prev_ref, inner_ref, outer_ref, param_ref, weight_ref,
    cols_ref, conv_ref, stats_ref, out_ref,
):
    parts = [ref[...] for ref in (part_ref, a_ref, b_ref, c_ref)]
    merged = stats_table(*merge(parts, 4 * LOCAL_COUNT))
    stats_ref[...] = merged
    wide = to_channels(merged)
    stats = [(wide[:, f : f + 1], wide[:, 4 + f : 5 + f]) for f in range(4)]
    active_columns(
        cols_ref, table_ref, stats, param_ref[:, 0:1], param_ref[:, 1:2], own_ref, prev_ref, inner_ref, outer_ref
    )

    def finish(h, total):
        for f in range(OWN):
            conv_ref[f, h] = total[:, f * W : (f + 1) * W]

    forward_conv(table_ref, weight_ref, cols_ref, finish)

    def row(f, h):
        return lambda: conv_ref[f, h]

    out_ref[...] = local_stats([[row(f, h) for h in range(ROWS)] for f in range(OWN)])


def merge_kernel(own_ref, a_ref, b_ref, c_ref, out_ref):
    mean, squares = merge([ref[...] for ref in (own_ref, a_ref, b_ref, c_ref)], LOCAL_COUNT)
    out_ref[...] = jnp.concatenate([mean, squares], axis=0)


def sum_kernel(own_ref, a_ref, b_ref, c_ref, out_ref):
    out_ref[...] = own_ref[...] + a_ref[...] + b_ref[...] + c_ref[...]


def turn(src_ref, dst_ref):
    row = lax.broadcasted_iota(jnp.int32, (C, C), 0)
    eye = (row == lax.broadcasted_iota(jnp.int32, (C, C), 1)).astype(BF16)
    for tap in range(27):
        k, spot = divmod(26 - tap, 9)
        block = lax.dot_general(
            eye, src_ref[:, tap * C : (tap + 1) * C], (((1,), (1,)), ((), ())), preferred_element_type=F32
        )
        dst_ref[k, :, spot * C : (spot + 1) * C] = block.astype(BF16)


def adjoint(table_ref, own_ref, next_ref, inner_ref, outer_ref, weight_ref, out_ref, cols_ref, turned_ref, first):
    for f in range(4):
        ends = beside(table_ref, inner_ref, outer_ref, first + f)
        for h in range(ROWS + 2):
            if h == 0:
                field = ends[0]
            elif h == ROWS + 1:
                field = ends[1]
            else:
                field = (own_ref if f < OWN else next_ref)[f % OWN, h - 1].astype(F32)
            store_shifted(cols_ref, h, f, field)
    turn(weight_ref, turned_ref)
    factors = [None] + [factor(table_ref, j, j) for j in (1, 2)]

    def finish(h, total):
        out_ref[0, h] = total[:, :W]
        out_ref[1, h] = total[:, W:]

    conv_rows([turned_ref[j] for j in range(3)], cols_ref, factors, finish)


def adjoint_two_kernel(
    table_ref, own_ref, next_ref, inner_ref, outer_ref, weight_ref, out_ref, cols_ref, turned_ref
):
    adjoint(table_ref, own_ref, next_ref, inner_ref, outer_ref, weight_ref, out_ref, cols_ref, turned_ref, 4)


def adjoint_one_kernel(
    table_ref, own_ref, next_ref, inner_ref, outer_ref, weight_ref, stats_ref, field_ref, param_ref,
    grad_ref, out_ref, cols_ref, turned_ref, upstream_ref,
):
    adjoint(
        table_ref, own_ref, next_ref, inner_ref, outer_ref, weight_ref, upstream_ref, cols_ref, turned_ref, 0
    )
    wide = to_channels(stats_ref[...])
    stats = [(wide[:, 2 + f : 3 + f], wide[:, 6 + f : 7 + f]) for f in range(OWN)]
    out_ref[...] = norm_grad(stats, field_ref, upstream_ref, param_ref, grad_ref, 0)


def norm_grad(stats, field_ref, upstream_ref, param_ref, grad_ref, place, active_ref=None):
    gain = jnp.broadcast_to(param_ref[:, place : place + 1], (C, W))
    bias = jnp.broadcast_to(param_ref[:, place + 1 : place + 2], (C, W))
    plain, weighted = [], []
    for f in range(OWN):
        mean = jnp.broadcast_to(stats[f][0], (C, W))
        inverse = jnp.broadcast_to(stats[f][1], (C, W))
        sums = None
        for h in range(ROWS):
            normalized = (field_ref[f, h].astype(F32) - mean) * inverse
            pre = normalized * gain + bias
            sigmoid = 1.0 / (1.0 + jnp.exp(-pre))
            grad = upstream_ref[f, h] * (sigmoid * (1.0 + pre * (1.0 - sigmoid))) * gain
            grad_ref[f, h] = grad
            if active_ref is not None:
                active_ref[f, h] = (pre * sigmoid).astype(BF16)
            pair = (grad, grad * normalized)
            sums = pair if sums is None else (sums[0] + pair[0], sums[1] + pair[1])
        plain.append(jnp.sum(sums[0], axis=1, keepdims=True))
        weighted.append(jnp.sum(sums[1], axis=1, keepdims=True))
    return to_groups(plain + weighted)


def norm_two_kernel(
    own_ref, a_ref, b_ref, c_ref, field_ref, upstream_ref, param_ref, active_ref, grad_ref, stats_ref, out_ref
):
    parts = [ref[...] for ref in (own_ref, a_ref, b_ref, c_ref)]
    merged = stats_table(*merge(parts, 4 * LOCAL_COUNT))
    stats_ref[...] = merged
    wide = to_channels(merged)
    stats = [(wide[:, f : f + 1], wide[:, 4 + f : 5 + f]) for f in range(OWN)]
    out_ref[...] = norm_grad(stats, field_ref, upstream_ref, param_ref, grad_ref, 2, active_ref)


def field_grad(stats, sums, grad_ref, field_ref, finish):
    totals = to_channels(sums * (1.0 / FULL_COUNT))
    for f in range(OWN):
        mean = jnp.broadcast_to(stats[f][0], (C, W))
        inverse = jnp.broadcast_to(stats[f][1], (C, W))
        plain = jnp.broadcast_to(totals[:, f : f + 1], (C, W))
        weighted = jnp.broadcast_to(totals[:, OWN + f : OWN + f + 1], (C, W))
        for h in range(ROWS):
            normalized = (field_ref[f, h].astype(F32) - mean) * inverse
            finish(f, h, inverse * (grad_ref[f, h] - plain - normalized * weighted))


def grad_conv_kernel(stats_ref, own_ref, a_ref, b_ref, c_ref, grad_ref, field_ref, out_ref):
    def finish(f, h, value):
        out_ref[f, h] = value.astype(BF16)

    wide = to_channels(stats_ref[...])
    stats = [(wide[:, f : f + 1], wide[:, 4 + f : 5 + f]) for f in range(OWN)]
    field_grad(stats, own_ref[...] + a_ref[...] + b_ref[...] + c_ref[...], grad_ref, field_ref, finish)


def input_grad_kernel(stats_ref, own_ref, a_ref, b_ref, c_ref, grad_ref, field_ref, cot_ref, out_ref, done_ref):
    def finish(f, h, value):
        out_ref[f, h] = (cot_ref[f, h].astype(F32) + value).astype(BF16)

    wide = to_channels(stats_ref[...])
    stats = [(wide[:, 2 + f : 3 + f], wide[:, 6 + f : 7 + f]) for f in range(OWN)]
    field_grad(stats, own_ref[...] + a_ref[...] + b_ref[...] + c_ref[...], grad_ref, field_ref, finish)
    done_ref[...] = jnp.zeros((8, W), F32)


def weight_kernel(table_ref, cols_ref, grad_ref, kept_ref, send_ref, dense_ref, turned_ref):
    for h in range(ROWS):
        for f in range(OWN):
            block = grad_ref[f, h].T
            start = (h * OWN + f) * W
            turned_ref[2, start : start + W, :] = block
            wide = block.astype(F32)
            for k in range(2):
                at = (2 - k) * 4 + f
                turned_ref[k, start : start + W, :] = (wide * table_ref[at : at + 1, 0:1]).astype(BF16)
    for k in range(3):
        for spot in range(9):
            start = spot * C
            rows = [
                cols_ref[h * TAP_ROWS + start : h * TAP_ROWS + start + C, k * W : (k + 2) * W]
                for h in range(ROWS)
            ]
            dense_ref[k * DEPTH + start : k * DEPTH + start + C, :] = jnp.dot(
                jnp.concatenate(rows, axis=1), turned_ref[k], preferred_element_type=F32
            )
    half = SHARE // 2
    first = jnp.broadcast_to(table_ref[14:15, :], (HALF, W)) < 0.5
    for s in range(SPACE):
        low = dense_ref[s * SHARE : (s + 1) * SHARE, 0:W]
        high = jnp.concatenate(
            [
                dense_ref[s * SHARE : s * SHARE + half, W:C],
                dense_ref[s * SHARE + half : (s + 1) * SHARE, W:C],
            ],
            axis=1,
        )
        spare = jnp.zeros((PACKED - SHARE - half, W), F32)
        packed = jnp.concatenate([low, high, spare], axis=0).astype(BF16)
        kept_ref[s] = jnp.where(first, packed[:HALF], packed[HALF:])
        send_ref[s] = jnp.where(first, packed[HALF:], packed[:HALF])


def conv_two_kernel(
    table_ref, own_ref, prev_ref, inner_ref, outer_ref, weight_ref, input_ref, decoded_ref, cols_ref
):
    for f in range(4):
        ends = beside(table_ref, inner_ref, outer_ref, f)
        for h in range(ROWS + 2):
            if h == 0:
                field = ends[0]
            elif h == ROWS + 1:
                field = ends[1]
            else:
                field = (prev_ref if f < OWN else own_ref)[f % OWN, h - 1].astype(F32)
            store_shifted(cols_ref, h, f, field)

    def finish(h, total):
        for f in range(OWN):
            field = input_ref[f, h].astype(F32) + total[:, f * W : (f + 1) * W]
            decoded_ref[f, h] = field.astype(BF16)

    forward_conv(table_ref, weight_ref, cols_ref, finish)


def pair_kernel(kept_one_ref, came_one_ref, kept_two_ref, came_two_ref, out_ref, done_ref):
    for i, (kept, came) in enumerate(((kept_one_ref, came_one_ref), (kept_two_ref, came_two_ref))):
        out_ref[:, i * HALF : (i + 1) * HALF] = (kept[...].astype(F32) + came[...].astype(F32)).astype(BF16)
    done_ref[...] = jnp.zeros((8, W), F32)


def gather_kernel(parts_ref, out_ref):
    for i in range(2):
        rows = slice(i * HALF, (i + 1) * HALF)
        total = parts_ref[0, rows].astype(F32)
        for s in range(1, SPACE):
            total = total + parts_ref[s, rows].astype(F32)
        out_ref[i] = total.astype(BF16)


def chips_kernel(place_ref, own_ref, a_ref, b_ref, c_ref, out_ref, room_ref):
    for d, ref in enumerate((own_ref, a_ref, b_ref, c_ref)):
        room_ref[lax.rem(place_ref[0] + d, CHIPS)] = ref[...]
    total = room_ref[0].astype(F32)
    for x in range(1, CHIPS):
        total = total + room_ref[x].astype(F32)
    out_ref[...] = total


def unpack_kernel(table_ref, own_ref, came_ref, *out_refs, scale):
    second = jnp.broadcast_to(table_ref[14:15, :], (HALF, W)) > 0.5
    half = SHARE // 2
    for i, out_ref in enumerate(out_refs):
        own, came = own_ref[i] * scale, came_ref[i] * scale
        packed = jnp.concatenate([jnp.where(second, came, own), jnp.where(second, own, came)], axis=0)
        high = packed[SHARE : SHARE + half]
        out_ref[0:W, :] = packed[0:SHARE].T
        out_ref[W:C, 0:half] = high[:, : C - W].T
        out_ref[W:C, half:SHARE] = high[:, C - W :].T


def table_kernel(lengths_ref, out_ref):
    place, row = lax.axis_index("tm"), lax.axis_index("space")
    ends, end = [], 0
    for i in range(CLIPS):
        end = end + lengths_ref[i]
        ends.append(end)

    def clip_of(frame):
        return sum((frame >= end).astype(jnp.int32) for end in ends)

    values = []
    for lag in range(3):
        for f in range(4):
            frame = place * OWN + f
            kept = (frame >= lag) & (clip_of(frame - lag) == clip_of(frame))
            values.append(kept.astype(F32) if lag else jnp.float32(1.0))
    flags = (row > 0, row < SPACE - 1, place % 2 > 0, row % 2 > 0)
    for i, value in enumerate(values + [flag.astype(F32) for flag in flags]):
        out_ref[i : i + 1, :] = jnp.full((1, W), value, F32)


FORWARD = [(i, i + 1) for i in range(TM - 1)]
BACKWARD = [(i + 1, i) for i in range(TM - 1)]
INNER = [(i, i ^ 1) for i in range(SPACE)]
OUTER = [(i, ((i - 1) ^ 1) + 1 if 0 < i < SPACE - 1 else SPACE - 1 - i) for i in range(SPACE)]
SIBLING = [(i, i ^ 1) for i in range(TM)]


def edge_rows(table, *blocks, after=()):
    rows = shape((OWN * len(blocks), C, W), BF16)
    return call(edges_kernel, (rows, rows), (table, *blocks), after=after)


def row_halos(inner, outer):
    return lax.ppermute(inner, "space", INNER), lax.ppermute(outer, "space", OUTER)


SIDE = 4


def along(part, stride):
    near = [
        [(i, i - (i // stride % SIDE) * stride + ((i // stride + d) % SIDE) * stride) for i in range(SPACE)]
        for d in range(1, SIDE)
    ]
    return (part, *(lax.ppermute(part, "space", route) for route in near))


def shape(dims, dtype=F32):
    return jax.ShapeDtypeStruct(dims, dtype)


FIELD = (OWN, ROWS, C, W)
COLS = (6 * TAP_ROWS, 4 * W)


def shards(
    activations,
    weight_one,
    weight_two,
    gain_one,
    bias_one,
    gain_two,
    bias_two,
    cotangent,
    clip_lengths,
):
    table = pl.pallas_call(
        table_kernel,
        out_shape=shape((16, W)),
        in_specs=[pl.BlockSpec(memory_space=pltpu.SMEM)],
        out_specs=pl.BlockSpec(memory_space=pltpu.VMEM),
        compiler_params=pltpu.CompilerParams(vmem_limit_bytes=1024 * 1024),
    )(clip_lengths)
    params = jnp.stack([gain_one, bias_one, gain_two, bias_two], axis=1)
    turned_one, turned_two = weight_one.T, weight_two.T
    small = shape((8, W))
    turned = pltpu.VMEM((3, C, DEPTH), BF16)
    packed = shape((SPACE, HALF, W), BF16)
    dense = [pltpu.VMEM((ALL_TAPS, C), F32), pltpu.VMEM((3, OWN * ROWS * W, C), BF16)]

    fields, part = call(stats_kernel, (shape(FIELD, BF16), small), (activations,))
    part, upstream = call(
        join_kernel, (small, shape(FIELD, BF16)), (lax.ppermute(part, "tm", FORWARD), part, cotangent)
    )
    previous = lax.ppermute(fields, "tm", FORWARD)
    following = lax.ppermute(upstream, "tm", BACKWARD)
    merged = call(merge_kernel, small, along(part, 1))
    parts_one = along(merged, SIDE)
    inner, outer = row_halos(*edge_rows(table, previous, fields, upstream, following, after=(merged,)))
    columns_one, conv_one, stats_one, part = call(
        conv_one_kernel,
        (shape(COLS, BF16), shape(FIELD), small, small),
        (table, *parts_one, fields, previous, inner, outer, params, turned_one),
        limit=12,
    )
    merged = call(merge_kernel, small, along(part, 1))
    parts_two = along(merged, SIDE)
    grad_active_two = call(
        adjoint_two_kernel,
        shape(FIELD),
        (table, upstream, following, inner, outer, turned_two),
        scratch=[pltpu.VMEM(COLS, BF16), turned],
        after=(merged,),
        limit=16,
    )
    active_two, grad_norm, stats_two, part = call(
        norm_two_kernel,
        (shape(FIELD, BF16), shape(FIELD), small, small),
        (*parts_two, conv_one, grad_active_two, params),
    )
    merged = call(sum_kernel, small, along(part, 1))
    sums_two = along(merged, SIDE)
    active_two = call(copy_kernel, shape(FIELD, BF16), (active_two,), after=(merged,))
    previous_two = lax.ppermute(active_two, "tm", FORWARD)
    grad_conv_one = call(grad_conv_kernel, shape(FIELD, BF16), (stats_two, *sums_two, grad_norm, conv_one))
    following_one = lax.ppermute(grad_conv_one, "tm", BACKWARD)
    edges_two = edge_rows(table, previous_two, active_two, after=(grad_conv_one,))
    inner_two, outer_two = row_halos(*edges_two)
    kept_one, sent_one = call(
        weight_kernel,
        (packed, packed),
        (table, columns_one, grad_conv_one),
        scratch=dense,
        after=(edges_two[0],),
        limit=16,
    )
    came_one = lax.ppermute(sent_one, "tm", SIBLING)
    edges_one = edge_rows(table, grad_conv_one, following_one, after=(sent_one,))
    inner_one, outer_one = row_halos(*edges_one)
    decoded, columns_two = call(
        conv_two_kernel,
        (shape(FIELD, BF16), shape(COLS, BF16)),
        (table, active_two, previous_two, inner_two, outer_two, turned_two, fields),
        after=(edges_one[0],),
        limit=12,
    )
    kept_two, sent_two = call(
        weight_kernel,
        (packed, packed),
        (table, columns_two, upstream),
        scratch=dense,
        after=(inner_one, outer_one),
        limit=16,
    )
    came_two = lax.ppermute(sent_two, "tm", SIBLING)
    pairs, done_pairs = call(
        pair_kernel,
        (shape((SPACE, PACKED, W), BF16), small),
        (kept_one, came_one, kept_two, came_two),
    )
    swapped = lax.all_to_all(pairs, "space", 0, 0)
    grad_norm, part = call(
        adjoint_one_kernel,
        (shape(FIELD), small),
        (table, grad_conv_one, following_one, inner_one, outer_one, turned_one, stats_one, fields, params),
        scratch=[pltpu.VMEM(COLS, BF16), turned, pltpu.VMEM(FIELD, F32)],
        after=(done_pairs,),
        limit=16,
    )
    merged = call(sum_kernel, small, along(part, 1))
    sums_one = along(merged, SIDE)
    half = call(gather_kernel, shape((2, HALF, W), BF16), (swapped,), after=sums_one[1:2])
    routes = [[(i, (i - 2 * d) % TM) for i in range(TM)] for d in range(1, CHIPS)]
    halves = (half, *(lax.ppermute(half, "tm", route) for route in routes))
    input_grad, done_grad = call(
        input_grad_kernel,
        (shape(FIELD, BF16), small),
        (stats_one, *sums_one, grad_norm, fields, upstream),
        us=3,
    )
    half = call(
        chips_kernel,
        shape((2, HALF, W)),
        ((lax.axis_index("tm") // 2).astype(jnp.int32).reshape(1), *halves),
        scratch=[pltpu.VMEM((CHIPS, 2, HALF, W), BF16)],
        smem=1,
        after=(done_grad,),
    )
    total_cells = OWN * TM * ROWS * SPACE * W
    share_one, share_two = call(
        functools.partial(unpack_kernel, scale=float(total_cells) ** -0.5),
        (shape((C, SHARE)),) * 2,
        (table, half, lax.ppermute(half, "tm", SIBLING)),
    )
    return (decoded, input_grad, share_one.T, share_two.T)


def solution(mesh):
    placed = (
        P("tm", "space", None, None),
        P(),
        P(),
        P(),
        P(),
        P(),
        P(),
        P("tm", "space", None, None),
        P(),
    )
    return jax.shard_map(
        shards,
        mesh=mesh,
        in_specs=placed,
        out_specs=(
            P("tm", "space", None, None),
            P("tm", "space", None, None),
            P("space", None),
            P("space", None),
        ),
        check_vma=False,
    )
```
